32 devices in a mesh: gx: 8 (over y, x, core), gy: 4 (over z).
Axes of the slice: x: 2, y: 2, z: 4, core: 2. Of those that a mesh axis runs over, the one named last changes fastest.
Arguments:
- in_table: float32 [32768, 300], P(('gx', 'gy')), may hold values from -3 to 3
- out_table: float32 [32768, 300], P(('gx', 'gy')), may hold values from -3 to 3
- hot_table: float32 [2048, 300], replicated, may hold values from -3 to 3
- centre_owner: int32 [3, 4096, 1], P(None, ('gx', 'gy')), may hold values from 0 to 31; in each aligned block of 128 rows (0 to 127, 128 to 255, ..., all dimensions but the last counted through in order) at most 8 rows name the same one
- centre_row: int32 [3, 4096], P(None, ('gx', 'gy')), may hold values from 0 to 1023
- bag_owner: int32 [3, 4096, 6], P(None, ('gx', 'gy')), may hold values from 0 to 31, all different within a row; in each aligned block of 128 rows (0 to 127, 128 to 255, ..., all dimensions but the last counted through in order) at most 48 rows name the same one
- bag_row: int32 [3, 4096, 6], P(None, ('gx', 'gy')), may hold values from 0 to 1023
- bag_len: int32 [3, 4096], P(None, ('gx', 'gy')), may hold values from 1 to 6
- context_owner: int32 [3, 4096, 1], P(None, ('gx', 'gy')), may hold values from 0 to 31; in each aligned block of 128 rows (0 to 127, 128 to 255, ..., all dimensions but the last counted through in order) at most 8 rows name the same one
- context_row: int32 [3, 4096], P(None, ('gx', 'gy')), may hold values from 0 to 1023
- negative_ids: int32 [3, 32768], P(None, ('gx', 'gy')), may hold values from 0 to 2047
Outputs:
- new_in_table: float32 [32768, 300], P(('gx', 'gy'))
- new_out_table: float32 [32768, 300], P(('gx', 'gy'))
- new_hot_table: float32 [2048, 300], replicated
The draws below stay inside these ranges and needn't reach their ends.
Inputs may be any that keep to these rules, and one draw needn't show every extreme that they name: `centre_owner`: in each step, the 128 centre words of one device name one owner at most 8 times, and some owner exactly that often. `bag_owner`: in each step, the bucket slots of one device's 128 centre words name one owner at most 48 times, and some owner exactly that often; the 6 slots of one word name distinct owners. Slots at positions bag_len and beyond are padding. `context_owner`: in each step, the 128 contexts of one device name one owner at most 8 times, and some owner exactly that often.
All inputs are finite; a program needn't handle non-finite values.
Results may differ from the reference program's by a relative error of at most 0.017.
Values sent between devices are 32-bit elements; how exact they have to be, the bound alone decides.
No kernel may reach another device: no remote copies, remote signals or barrier semaphores. Data moves between devices by JAX's collectives and lax.ppermute only.
A program may use at most 128 MiB of HBM per device.

```python
import math
import jax
import jax.numpy as jnp
import numpy as np
from jax import lax

D = 300
TOK_DEV = 128
NEG = 1024
ROWS_DEV = 1024
OUT_DEV = 1024
HOT = 2048
BAG = 6
STEPS = 3
OWNERS = 32
TOKENS = 4096
NEGS = 32768
ROWS = 32768
OUT_ROWS = 32768
CAP_C = 8
CAP_B = 48
N_GX = 8
N_GY = 4


def set_ends(values, rng, least, high):
    dims = values.shape
    index_at = [jax.random.randint(jax.random.fold_in(rng, axis), (), 0, dims[axis]) for axis in range(len(dims))]
    values = values.at[tuple(index_at)].set(least)
    longest = dims.index(max(dims))
    index_at[longest] = (index_at[longest] + 1) % dims[longest]
    return values.at[tuple(index_at)].set(high)


def steps_of(stream_key, shape, split, smallest, top_value):
    factor_of = 1.0
    for axis_at, blocks in split:
        draws = jax.random.uniform(jax.random.fold_in(jax.random.fold_in(stream_key, 6), axis_at), (blocks,), jnp.float32, smallest / len(split), top_value / len(split))
        factor_of = factor_of * jnp.repeat(jnp.exp(draws), shape[axis_at] // blocks).reshape((-1,) + (1,) * (len(shape) - 1 - axis_at))
    return factor_of


def rank_bounds(count, lean):
    weights = [(1 << 20) // math.isqrt(rank ** lean) + 1 for rank in range(1, count + 1)]
    scale = 1 + sum(weights) // (1 << 30)
    return np.cumsum(np.array([max(1, weight // scale) for weight in weights]))


def skewed_ids(stream_key, extent, number_of, lean):
    listing = rank_bounds(number_of, lean)
    lot = jax.random.randint(jax.random.fold_in(stream_key, 1), extent, 0, int(listing[number_of - 1]))
    rank = jnp.searchsorted(jnp.asarray(listing, jnp.int32), lot, side="right")
    return jax.random.permutation(jax.random.fold_in(stream_key, 2), number_of)[rank].astype(jnp.int32)


def deal_out(own_key, own, number, rows, amount, top, reach, slope):
    sequence = jax.random.permutation(own_key, amount)
    heavy_load, ordinary = load_shares(amount, rows * top, reach, slope, True), load_shares(amount, rows * top, reach, slope, False)
    places = jnp.arange(amount)

    def named(tallies, offset_by):
        used = int((tallies > 0).sum())
        fixed = max(1, used // 4)
        passed = fixed + (places - fixed + offset_by * (used - fixed)) % max(1, amount - fixed)
        return jnp.zeros((amount,), jnp.int32).at[sequence[jnp.where(places < fixed, places, passed)]].set(jnp.asarray(tallies, jnp.int32))

    tallies = jnp.where(number % 4 == 0, named(heavy_load, number // 4), named(ordinary, number - number // 4 - 1))
    mixed = jax.random.permutation(jax.random.fold_in(own, 3), amount)
    source_of, taker = mixed[0:amount // 2 * 2:2], mixed[1:amount // 2 * 2:2]
    margin = jnp.minimum(tallies[source_of] - 1, reach - tallies[taker]) // 2
    margin = jnp.where((source_of == sequence[0]) | (taker == sequence[0]) | (tallies[taker] == 0), 0, jnp.maximum(margin, 0))
    passed = jax.random.randint(jax.random.fold_in(own, 4), (amount // 2,), 0, 1 << 20) % (margin + 1)
    tallies = tallies.at[source_of].add(-passed).at[taker].add(passed)
    members = jnp.searchsorted(jnp.cumsum(tallies), jnp.arange(rows * top), side="right").astype(jnp.int32)
    listing = members.reshape(top, rows).T
    listing = listing[jax.random.permutation(jax.random.fold_in(own, 1), rows)]
    offset_by = jax.random.randint(jax.random.fold_in(own, 2), (rows, 1), 0, top)
    return jnp.take_along_axis(listing, (jnp.arange(top)[None, :] + offset_by) % top, axis=1)


def load_shares(count, total, reach, slope, full):
    loads = [(1 << 20) // math.isqrt(standing ** slope) + 1 for standing in range(1, count + 1)]
    largest = reach if full else min(reach, max(-(-total // count), total * loads[0] // sum(loads)))
    least = 1 if total - largest >= count - 1 else 0
    given, surplus = [largest] + [least] * (count - 1), total - largest - least * (count - 1)
    while surplus > 0:
        free = [i for i in range(1, count) if given[i] < largest] or [i for i in range(1, count) if given[i] < reach]
        pool, budget = sum([loads[i] for i in free]), surplus
        for i in free:
            more = min(reach - given[i], max(1, budget * loads[i] // pool), surplus)
            given[i] = given[i] + more
            surplus = surplus - more
    return np.array(given)


def centred(stream_key, shape, spread, most, shards=(), kind=jnp.bfloat16):
    drawn = jax.random.normal(stream_key, shape, jnp.float32) * spread
    if len(shards) > 0:
        drawn = steps_of(stream_key, shape, shards, -0.22, 0.18) * drawn
    return jnp.clip(drawn, min=-most, max=most).astype(kind)


def setup_inputs(seed: int = 0) -> dict:
    key_of = jax.random.split(jax.random.key(seed), 12)
    in_table = centred(key_of[0], (ROWS, D), 0.5, 3.0, ((0, 32),), jnp.float32)
    out_table = centred(key_of[1], (OUT_ROWS, D), 0.5, 3.0, ((0, 32),), jnp.float32)
    hot_table = centred(key_of[2], (HOT, D), 0.5, 3.0, (), jnp.float32)
    centre_owner_keys = jax.random.split(jax.random.fold_in(key_of[3], 1), STEPS * TOKENS // TOK_DEV)
    centre_owner_turns = jax.random.permutation(jax.random.fold_in(key_of[3], 3), STEPS * TOKENS // TOK_DEV)
    centre_owner = jax.vmap(lambda own, number: deal_out(jax.random.fold_in(key_of[3], 2), own, number, TOK_DEV, OWNERS, 1, CAP_C, 1))(centre_owner_keys, centre_owner_turns).reshape((STEPS, TOKENS, 1))
    centre_row = set_ends(jax.random.randint(key_of[4], (STEPS, TOKENS), 0, ROWS_DEV), jax.random.fold_in(key_of[4], 1), 0, ROWS_DEV - 1).astype(jnp.int32)
    bag_owner_keys = jax.random.split(jax.random.fold_in(key_of[5], 1), STEPS * TOKENS // TOK_DEV)
    bag_owner_turns = jax.random.permutation(jax.random.fold_in(key_of[5], 3), STEPS * TOKENS // TOK_DEV)
    bag_owner = jax.vmap(lambda own, number: deal_out(jax.random.fold_in(key_of[5], 2), own, number, TOK_DEV, OWNERS, BAG, CAP_B, 1))(bag_owner_keys, bag_owner_turns).reshape((STEPS, TOKENS, BAG))
    bag_row = set_ends(jax.random.randint(key_of[6], (STEPS, TOKENS, BAG), 0, ROWS_DEV), jax.random.fold_in(key_of[6], 1), 0, ROWS_DEV - 1).astype(jnp.int32)
    bag_len = set_ends(jax.random.randint(key_of[7], (STEPS, TOKENS), 1, BAG + 1), jax.random.fold_in(key_of[7], 1), 1, BAG).astype(jnp.int32)
    context_owner_keys = jax.random.split(jax.random.fold_in(key_of[8], 1), STEPS * TOKENS // TOK_DEV)
    context_owner_turns = jax.random.permutation(jax.random.fold_in(key_of[8], 3), STEPS * TOKENS // TOK_DEV)
    context_owner = jax.vmap(lambda own, number: deal_out(jax.random.fold_in(key_of[8], 2), own, number, TOK_DEV, OWNERS, 1, CAP_C, 1))(context_owner_keys, context_owner_turns).reshape((STEPS, TOKENS, 1))
    context_row = set_ends(jax.random.randint(key_of[9], (STEPS, TOKENS), 0, OUT_DEV), jax.random.fold_in(key_of[9], 1), 0, OUT_DEV - 1).astype(jnp.int32)
    negative_ids = set_ends(skewed_ids(key_of[10], (STEPS, NEGS), HOT, 2), jax.random.fold_in(key_of[10], 3), 0, HOT - 1).astype(jnp.int32)
    return dict(in_table=in_table, out_table=out_table, hot_table=hot_table, centre_owner=centre_owner, centre_row=centre_row, bag_owner=bag_owner, bag_row=bag_row, bag_len=bag_len, context_owner=context_owner, context_row=context_row, negative_ids=negative_ids)


learn_rate = 2.0
exact = lax.Precision.HIGHEST


def fetch_rows(table, row_ids):
    return table[row_ids]


def score_block(pair):
    centre_part, negative_part = pair
    scores = jnp.dot(centre_part, negative_part.T, precision=exact, preferred_element_type=jnp.float32)
    neg_grad = (16.0 / NEG) * jax.nn.sigmoid(scores)
    toward_centre = jnp.dot(neg_grad, negative_part, precision=exact, preferred_element_type=jnp.float32)
    toward_negative = jnp.dot(neg_grad.T, centre_part, precision=exact, preferred_element_type=jnp.float32)
    return toward_centre, toward_negative


def reference(in_table, out_table, hot_table, centre_owner, centre_row, bag_owner, bag_row, bag_len, context_owner, context_row, negative_ids):
    owners = N_GX * N_GY
    for step_index in range(STEPS):
        centre_ids = (centre_owner[step_index, :, 0] * ROWS_DEV + centre_row[step_index]).astype(jnp.int32)
        bucket_ids = (bag_owner[step_index] * ROWS_DEV + bag_row[step_index]).astype(jnp.int32).reshape(-1)
        context_ids = (context_owner[step_index, :, 0] * OUT_DEV + context_row[step_index]).astype(jnp.int32)
        word_vec = fetch_rows(in_table, centre_ids)
        bag_vec = fetch_rows(in_table, bucket_ids).reshape(TOKENS, BAG, D)
        context_vec = fetch_rows(out_table, context_ids)
        kept = (jnp.arange(BAG, dtype=jnp.int32)[None, :] < bag_len[step_index][:, None]).astype(jnp.float32)
        denom = 1.0 + bag_len[step_index].astype(jnp.float32)
        centre_vec = (word_vec + jnp.sum(bag_vec * kept[:, :, None], axis=1)) / denom[:, None]
        negatives = hot_table[negative_ids[step_index]]
        positive = jnp.sum(centre_vec * context_vec, axis=1)
        pos_grad = jax.nn.sigmoid(positive) - 1.0
        toward_centre, toward_negative = lax.map(score_block, (centre_vec.reshape(owners, TOK_DEV, D), negatives.reshape(owners, NEG, D)))
        centre_grad = pos_grad[:, None] * context_vec + toward_centre.reshape(TOKENS, D)
        word_grad = centre_grad / denom[:, None]
        bag_grad = kept[:, :, None] * centre_grad[:, None, :] / denom[:, None, None]
        in_total = jnp.zeros(in_table.shape, jnp.float32).at[centre_ids].add(word_grad)
        in_total = in_total.at[bucket_ids].add(bag_grad.reshape(-1, D))
        out_total = jnp.zeros(out_table.shape, jnp.float32).at[context_ids].add(pos_grad[:, None] * centre_vec)
        hot_total = jnp.zeros(hot_table.shape, jnp.float32).at[negative_ids[step_index]].add(toward_negative.reshape(-1, D))
        in_table = in_table - learn_rate * in_total
        out_table = out_table - learn_rate * out_total
        hot_table = hot_table - learn_rate * hot_total
    return in_table, out_table, hot_table
```

```python
import functools
import jax
import jax.numpy as jnp
from jax import lax
from jax.experimental import pallas as pl
from jax.experimental.pallas import tpu as pltpu
from jax.sharding import PartitionSpec as P

learn_rate = 2.0
exact = lax.Precision.HIGHEST
axes = ("gx", "gy")
LANES = 128
META = 16
SLOTS = 8
f32, bf16, i32 = jnp.float32, jnp.bfloat16, jnp.int32
NT = (((1,), (1,)), ((), ()))
TN = (((0,), (0,)), ((), ()))


def swap(x, bit, devices):
    return lax.ppermute(x, axes, [(d, d ^ bit) for d in range(devices)])


def split3(x):
    hi = x.astype(bf16)
    rest = x - hi.astype(f32)
    mid = rest.astype(bf16)
    return hi, mid, (rest - mid.astype(f32)).astype(bf16)


def split2(x):
    hi = x.astype(bf16)
    return hi, (x - hi.astype(f32)).astype(bf16)


class Tree:
    def __init__(self, gx, gy):
        self.gx, self.gy = gx, gy
        self.devices = gx * gy
        self.low = [1 << b for b in range(gy.bit_length() - 1)]
        self.high = [gy << b for b in range(1, gx.bit_length() - 1)]
        self.core = gy

    def widen(self, x, bits, descending):
        m = len(bits)
        x = x.reshape((1,) * m + x.shape)
        order = list(range(m))
        if descending:
            order.reverse()
        for b in order:
            x = jnp.concatenate([x, swap(x, bits[b], self.devices)], axis=m - 1 - b)
        return x.reshape((-1,) + x.shape[m + 1:])

    def gather(self, a, b):
        out = []
        for part, descending in ((a, False), (b, True)):
            x = self.widen(part[None], self.low, False)
            x = self.widen(x, self.high, descending)
            out += [x, swap(x, self.core, self.devices)]
        return out

    def gather_gx(self, a, b):
        out = []
        for part, descending in ((a, False), (b, True)):
            x = self.widen(part[None], self.high, descending)
            out += [x, swap(x, self.core, self.devices)]
        return out

    def gather_one(self, x):
        x = self.widen(x[None], self.low, False)
        x = self.widen(x, self.high, False)
        return jnp.concatenate([x, swap(x, self.core, self.devices)], axis=0)

    def reduce(self, keep, send, descending):
        x = keep + swap(send, self.core, self.devices)
        m = len(self.high)
        x = x.reshape((2,) * m + (self.gy,) + x.shape[1:])
        order = list(range(m))
        if descending:
            order.reverse()
        for b in order:
            axis = m - 1 - b
            near = lax.slice_in_dim(x, 0, 1, axis=axis)
            far = lax.slice_in_dim(x, 1, 2, axis=axis)
            x = near + swap(far, self.high[b], self.devices)
        x = x.reshape(x.shape[m:])
        for bit in reversed(self.low):
            half = x.shape[0] // 2
            x = x[:half] + swap(x[half:], bit, self.devices)
        return x[0]

    def place_of(self, mask):
        bits = self.devices.bit_length() - 1
        g, low = mask // self.gy, mask % self.gy
        return (g % 2) * (1 << (bits - 1)) + (g // 2) * self.gy + low

    def slice_mask(self, place):
        half = self.gx // 2
        return place // half + 2 * (place % half)


def params(*semantics):
    return pltpu.CompilerParams(dimension_semantics=semantics, vmem_limit_bytes=40 * 2**20)


def cost(flops, nbytes, trans=0):
    return pl.CostEstimate(flops=int(flops), bytes_accessed=int(nbytes), transcendentals=int(trans))


def lane_pair(ref0, ref1):
    return jnp.concatenate([ref0[0], ref1[0]], axis=1)


def count_kernel(width, offset_ref, ids_ref, out_ref):
    offset = offset_ref[pl.program_id(1)]
    ids = ids_ref[0, 0, SLOTS:, :] - offset
    hot = lax.broadcasted_iota(i32, (width, LANES), 0)
    total = jnp.zeros((8, width), f32)
    ones = jnp.ones((8, LANES), bf16)
    for k in range(META - SLOTS):
        same = (hot == ids[k:k + 1, :]).astype(f32).astype(bf16)
        total = total + lax.dot_general(ones, same, NT, preferred_element_type=f32)
    out_ref[0, 0] = total[0:1, :]


def count(meta, offsets, width, ids_index):
    steps = meta.shape[1]
    places = offsets.shape[0]
    return pl.pallas_call(
        functools.partial(count_kernel, width),
        out_shape=jax.ShapeDtypeStruct((steps, places, 1, width), f32),
        grid_spec=pltpu.PrefetchScalarGridSpec(
            num_scalar_prefetch=1,
            grid=(steps, places),
            in_specs=[pl.BlockSpec((1, 1, META, LANES), ids_index)],
            out_specs=pl.BlockSpec((1, 1, 1, width), lambda s, p, o: (s, p, 0, 0)),
        ),
        compiler_params=params("arbitrary", "arbitrary"),
        cost_estimate=cost(steps * places * 2 * 8 * width * 1024, steps * places * 8192),
        name="count",
    )(offsets, meta)


def couple_kernel(own_ref, other_ref, in_ref, out_ref, wide):
    @pl.when(pl.program_id(0) == 0)
    def _():
        for k in range(SLOTS):
            wide[k] = jnp.broadcast_to(own_ref[0, :, k:k + 1], wide.shape[1:])

    for c in range(2):
        total = jnp.zeros(wide.shape[1:], f32)
        for k in range(SLOTS - 1):
            row = other_ref[c, 0, 0, k:k + 1, :]
            in_bag = wide[1] == row
            for j in range(2, SLOTS - 1):
                in_bag = in_bag | (wide[j] == row)
            total = total + jnp.where(in_bag, 1.0, 0.0) + jnp.where(wide[0] == row, 1.0, 0.0)
        in_ref[c, 0] = total.astype(bf16)
        same = wide[SLOTS - 1] == other_ref[c, 0, 0, SLOTS - 1:SLOTS, :]
        out_ref[c, 0] = jnp.where(same, 1.0, 0.0).astype(bf16)


def couple(own, meta, later, earlier):
    half, n = meta.shape[1], own.shape[1]
    shape = jax.ShapeDtypeStruct((2, half, n, n), bf16)
    spec = pl.BlockSpec((2, 1, n, n), lambda p: (0, p, 0, 0))
    return pl.pallas_call(
        couple_kernel,
        out_shape=(shape, shape),
        grid=(half,),
        in_specs=[
            pl.BlockSpec((1, n, SLOTS), lambda p: (later, 0, 0)),
            pl.BlockSpec((2, 1, 1, META, LANES), lambda p: (0, p, earlier, 0, 0)),
        ],
        out_specs=(spec, spec),
        scratch_shapes=[pltpu.VMEM((SLOTS, n, n), i32)],
        compiler_params=params("arbitrary"),
        cost_estimate=cost(half * 2 * n * n * 150, half * n * n * 8),
        name="couple",
    )(own, meta)


def chosen(ref, base, rows, context):
    parts = []
    for c in range(2):
        ids = ref[c, 0, 0, :SLOTS, :] - base
        lane_iota = lax.broadcasted_iota(i32, (rows, LANES), 0)
        if context:
            parts.append(jnp.where(lane_iota == ids[SLOTS - 1:, :], 1.0, 0.0))
        else:
            ids = jnp.where((ids >= 0) & (ids < rows), ids, -1)
            bag = jnp.max(ids[1:SLOTS - 1, :], axis=0, keepdims=True)
            parts.append(jnp.where(lane_iota == ids[0:1, :], 1.0, 0.0) + jnp.where(lane_iota == bag, 1.0, 0.0))
    return jnp.concatenate(parts, axis=1).astype(bf16)


def base_kernel(rows, base_ref, meta_ref, table_ref, a0, a1, b0, b1, parts):
    @pl.when(pl.program_id(0) == 0)
    def _():
        for k, part in enumerate(split3(table_ref[...])):
            parts[k] = part

    pick = chosen(meta_ref, base_ref[0], rows, False)
    total = jnp.dot(parts[0], pick, preferred_element_type=f32)
    for k in (1, 2):
        total = total + jnp.dot(parts[k], pick, preferred_element_type=f32)
    h = a0.shape[1]
    a0[0] = total[:h, :LANES]
    a1[0] = total[:h, LANES:]
    b0[0] = total[h:, :LANES]
    b1[0] = total[h:, LANES:]


def base_sums(table_t, meta, base, step):
    half = meta.shape[1]
    feats, rows = table_t.shape
    shape = jax.ShapeDtypeStruct((half, feats // 2, LANES), f32)
    spec = pl.BlockSpec((1, feats // 2, LANES), lambda p, b: (p, 0, 0))
    return pl.pallas_call(
        functools.partial(base_kernel, rows),
        out_shape=(shape,) * 4,
        grid_spec=pltpu.PrefetchScalarGridSpec(
            num_scalar_prefetch=1,
            grid=(half,),
            in_specs=[
                pl.BlockSpec((2, 1, 1, META, LANES), lambda p, b: (0, p, step, 0, 0)),
                pl.BlockSpec((feats, rows), lambda p, b: (0, 0)),
            ],
            out_specs=(spec,) * 4,
            scratch_shapes=[pltpu.VMEM((3, feats, rows), bf16)],
        ),
        compiler_params=params("arbitrary"),
        cost_estimate=cost(2 * 3 * half * 256 * feats * rows, half * 2 * feats * 512 + feats * rows * 4),
        name="base_sums",
    )(base, meta, table_t)


def update_kernel(rows, context, base_ref, meta_ref, table_ref, *refs):
    out_ref = refs[-1]
    ga0, ga1, gb0, gb1 = refs[:4]

    @pl.when(pl.program_id(0) == 0)
    def _():
        out_ref[...] = table_ref[...]

    pick = chosen(meta_ref, base_ref[0], rows, context)
    h = ga0.shape[1]
    if context:
        ca0, ca1, cb0, cb1, pos_row = refs[4], refs[5], refs[6], refs[7], refs[8]
        del pos_row
    halves = [lane_pair(ga0, ga1), lane_pair(gb0, gb1)]
    if context:
        at = out_ref.shape[0] - 4 - h
        pos = halves[1][at:at + 1, :]
        halves = [lane_pair(ca0, ca1) * pos, lane_pair(cb0, cb1) * pos]
    for k in range(2):
        part = jnp.zeros((h, rows), f32)
        for piece in split2(halves[k] * learn_rate):
            part = part + lax.dot_general(piece, pick, NT, preferred_element_type=f32)
        out_ref[k * h:(k + 1) * h, :] = out_ref[k * h:(k + 1) * h, :] - part


def update(table_t, meta, base, step, g, c=None):
    half = meta.shape[1]
    feats, rows = table_t.shape
    piece = pl.BlockSpec((1, feats // 2, LANES), lambda p, b: (p, 0, 0))
    whole = pl.BlockSpec((feats, rows), lambda p, b: (0, 0))
    context = c is not None
    arrays = list(g) + (list(c) if context else [])
    kernel = functools.partial(context_update_kernel if context else update_kernel, rows, context)
    return pl.pallas_call(
        kernel,
        out_shape=jax.ShapeDtypeStruct((feats, rows), f32),
        grid_spec=pltpu.PrefetchScalarGridSpec(
            num_scalar_prefetch=1,
            grid=(half,),
            in_specs=[pl.BlockSpec((2, 1, 1, META, LANES), lambda p, b: (0, p, step, 0, 0)), whole]
            + [piece] * len(arrays),
            out_specs=whole,
        ),
        compiler_params=params("arbitrary"),
        cost_estimate=cost(2 * 2 * half * 256 * feats * rows, half * 2 * feats * 512 * len(arrays) // 4),
        name="context_update" if context else "update",
    )(base, meta, table_t, *arrays)


def context_update_kernel(rows, context, base_ref, meta_ref, table_ref, *refs):
    update_kernel(rows, context, base_ref, meta_ref, table_ref, *refs[:8], None, refs[8])


def absorb_kernel(width, ga0, ga1, gb0, gb1, ca0, ca1, cb0, cb1, in_ref, ctx_ref, c_out, x_out):
    @pl.when(pl.program_id(0) == 0)
    def _():
        c_out[...] = jnp.zeros_like(c_out)
        x_out[...] = jnp.zeros_like(x_out)

    h = ga0.shape[1]
    in_pair = jnp.concatenate([in_ref[0, 0], in_ref[1, 0]], axis=1)
    ctx_pair = jnp.concatenate([ctx_ref[0, 0], ctx_ref[1, 0]], axis=1)
    ga, gb = lane_pair(ga0, ga1), lane_pair(gb0, gb1)
    pos = gb[width - h:width - h + 1, :]
    for k, (grad, centre) in enumerate(((ga, lane_pair(ca0, ca1)), (gb, lane_pair(cb0, cb1)))):
        at = pl.ds(k * h, h)
        part = jnp.zeros((h, c_out.shape[1]), f32)
        for piece in split3(grad * learn_rate):
            part = part + lax.dot_general(piece, in_pair, NT, preferred_element_type=f32)
        c_out[at, :] += part
        part = jnp.zeros((h, c_out.shape[1]), f32)
        for piece in split3(centre * pos * learn_rate):
            part = part + lax.dot_general(piece, ctx_pair, NT, preferred_element_type=f32)
        x_out[at, :] += part


def absorb(width, g, c, in_pairs, ctx_pairs):
    half, feats_half, n = g[0].shape
    piece = pl.BlockSpec((1, feats_half, n), lambda p: (p, 0, 0))
    pair = pl.BlockSpec((2, 1, n, n), lambda p: (0, p, 0, 0))
    shape = jax.ShapeDtypeStruct((2 * feats_half, n), f32)
    spec = pl.BlockSpec((2 * feats_half, n), lambda p: (0, 0))
    return pl.pallas_call(
        functools.partial(absorb_kernel, width),
        out_shape=(shape, shape),
        grid=(half,),
        in_specs=[piece] * 8 + [pair] * 2,
        out_specs=(spec, spec),
        compiler_params=params("arbitrary"),
        cost_estimate=cost(2 * 2 * 3 * half * 256 * feats_half * 2 * n, half * 256 * feats_half * 16),
        name="absorb",
    )(*g, *c, in_pairs, ctx_pairs)


def own_kernel(width, scale, c_ref, x_ref, denom_ref, cnt_ref, a0, a1, b0, b1, out_ref, total):
    p = pl.program_id(0)

    @pl.when(p == 0)
    def _():
        total[...] = jnp.zeros_like(total)

    centre = c_ref[...]
    for c, (a, b) in enumerate(((a0, b0), (a1, b1))):
        hot = jnp.concatenate([a[0], b[0]], axis=0)
        scores = lax.dot_general(centre, hot, TN, precision=exact, preferred_element_type=f32)
        grad = (scale * cnt_ref[0, c, 0]) * jax.nn.sigmoid(scores)
        total[...] += lax.dot_general(hot, grad, NT, precision=exact, preferred_element_type=f32)

    @pl.when(p == pl.num_programs(0) - 1)
    def _():
        context = x_ref[...]
        positive = jnp.sum(centre * context, axis=0, keepdims=True)
        pos = jax.nn.sigmoid(positive) - 1.0
        grad = (pos * context + total[...]) / denom_ref[...]
        feature = lax.broadcasted_iota(i32, grad.shape, 0)
        out_ref[...] = jnp.where(feature == width, pos, grad)


def own_grads(width, scale, centre, context, denom, cnt, hot):
    feats, n = centre.shape
    half, feats_half, hot_slice = hot[0].shape
    whole = pl.BlockSpec((feats, n), lambda p: (0, 0))
    piece = pl.BlockSpec((1, feats_half, hot_slice), lambda p: (p, 0, 0))
    return pl.pallas_call(
        functools.partial(own_kernel, width, scale),
        out_shape=jax.ShapeDtypeStruct((feats, n), f32),
        grid=(half,),
        in_specs=[
            whole,
            whole,
            pl.BlockSpec((1, n), lambda p: (0, 0)),
            pl.BlockSpec((1, 2, 1, 1, hot_slice), lambda p: (0, 0, p, 0, 0)),
        ]
        + [piece] * 4,
        out_specs=whole,
        scratch_shapes=[pltpu.VMEM((feats, n), f32)],
        compiler_params=params("arbitrary"),
        cost_estimate=cost(2 * 2 * 6 * half * 2 * hot_slice * feats * n, half * 4 * feats_half * hot_slice * 4),
        name="own_grads",
    )(centre, context, denom, cnt, *hot)


def hot_kernel(scale, cnt_ref, hot_a, hot_b, a0, a1, b0, b1, out_a, out_b, total):
    p = pl.program_id(0)

    @pl.when(p == 0)
    def _():
        total[...] = jnp.zeros_like(total)

    hot = jnp.concatenate([hot_a[0], hot_b[0]], axis=0)
    for c, (a, b) in enumerate(((a0, b0), (a1, b1))):
        centre = jnp.concatenate([a[0], b[0]], axis=0)
        scores = lax.dot_general(centre, hot, TN, precision=exact, preferred_element_type=f32)
        grad = (scale * cnt_ref[0, c, 0]) * jax.nn.sigmoid(scores)
        total[...] += jnp.dot(centre, grad, precision=exact, preferred_element_type=f32)

    @pl.when(p == pl.num_programs(0) - 1)
    def _():
        h = out_a.shape[0]
        out_a[...] = hot_a[0] - learn_rate * total[:h, :]
        out_b[...] = hot_b[0] - learn_rate * total[h:, :]


def hot_update(scale, cnt, hot, c):
    half, feats_half, n = c[0].shape
    hot_slice = hot[0].shape[2]
    shape = jax.ShapeDtypeStruct((feats_half, hot_slice), f32)
    out = pl.BlockSpec((feats_half, hot_slice), lambda p: (0, 0))
    first = pl.BlockSpec((1, feats_half, hot_slice), lambda p: (0, 0, 0))
    piece = pl.BlockSpec((1, feats_half, n), lambda p: (p, 0, 0))
    return pl.pallas_call(
        functools.partial(hot_kernel, scale),
        out_shape=(shape, shape),
        grid=(half,),
        in_specs=[pl.BlockSpec((1, 2, 1, 1, hot_slice), lambda p: (0, 0, p, 0, 0)), first, first] + [piece] * 4,
        out_specs=(out, out),
        scratch_shapes=[pltpu.VMEM((2 * feats_half, hot_slice), f32)],
        compiler_params=params("arbitrary"),
        cost_estimate=cost(2 * 2 * 6 * half * 256 * hot_slice * feats_half * 2, half * 256 * feats_half * 8),
        name="hot_update",
    )(cnt, hot[0], hot[2], *c)


def fetch_contexts(tree, me, out_table, meta_flat, owner, cap):
    rows, width = out_table.shape
    devices, steps = meta_flat.shape[0], meta_flat.shape[1]
    n = owner.shape[1]
    ids = meta_flat[:, :, SLOTS - 1, :] - me * rows
    mine = (ids >= 0) & (ids < rows)
    before = jnp.triu(jnp.ones((n, n), bf16), 1)
    rank = jnp.dot(mine.astype(bf16), before, preferred_element_type=f32).astype(i32)
    slots = jnp.arange(cap, dtype=i32)
    hit = mine[:, :, None, :] & (rank[:, :, None, :] == slots[None, None, :, None])
    wanted = jnp.sum(jnp.where(hit, ids[:, :, None, :], 0), axis=3)
    order = tree.place_of(me ^ jnp.arange(devices, dtype=i32))
    wanted = wanted[order].reshape(devices, steps * cap)
    got = lax.all_to_all(out_table[wanted], axes, split_axis=0, concat_axis=0, tiled=True)
    same = (owner[:, :, None] == owner[:, None, :]) & (
        jnp.arange(n)[None, :, None] > jnp.arange(n)[None, None, :]
    )
    own_rank = jnp.sum(same.astype(i32), axis=2)
    at = (owner * steps + jnp.arange(steps, dtype=i32)[:, None]) * cap + own_rank
    return got.reshape(devices * steps * cap, width)[at]


def body(
    in_table,
    out_table,
    hot_table,
    centre_owner,
    centre_row,
    bag_owner,
    bag_row,
    bag_len,
    context_owner,
    context_row,
    negative_ids,
):
    gx, gy = lax.axis_size("gx"), lax.axis_size("gy")
    tree = Tree(gx, gy)
    devices = tree.devices
    me_x = lax.axis_index("gx").astype(i32)
    me = me_x * gy + lax.axis_index("gy").astype(i32)
    steps, n, bag = bag_row.shape
    rows, width = in_table.shape
    out_rows = out_table.shape[0]
    hot_rows = hot_table.shape[0]
    neg = negative_ids.shape[1]
    cap = max(2, 2 * n // devices)
    hot_slice = hot_rows // gx
    feats = -(-(width + 1) // 16) * 16
    h = feats // 2
    scale = 16.0 / neg

    kept = jnp.arange(bag, dtype=i32)[None, None, :] < bag_len[:, :, None]
    centre_ids = centre_owner * rows + centre_row[:, :, None]
    bag_ids = bag_owner * rows + bag_row
    context_ids = context_owner * out_rows + context_row[:, :, None]
    own = jnp.concatenate([centre_ids, jnp.where(kept, bag_ids, -2), context_ids], axis=2)
    sent = jnp.concatenate([centre_ids, jnp.where(kept, bag_ids, -1), context_ids], axis=2)
    meta = jnp.concatenate(
        [jnp.swapaxes(sent, 1, 2), negative_ids.reshape(steps, META - SLOTS, LANES)], axis=1
    )
    meta_flat = tree.gather_one(meta.reshape(steps * META, LANES)).reshape(devices, steps, META, LANES)
    meta_all = meta_flat.reshape(2, devices // 2, steps, META, LANES)

    in_base = (me * rows).reshape(1)
    out_base = (me * out_rows).reshape(1)
    spare = ((0, feats - width), (0, 0))
    in_t = jnp.pad(in_table.T, spare)
    out_t = jnp.pad(out_table.T, spare)
    slice_of = me_x ^ tree.slice_mask(jnp.arange(gx, dtype=i32))
    hot_t = jnp.pad(hot_table, ((0, 0), (0, feats - width))).reshape(gx, hot_slice, feats)
    hot_t = jnp.swapaxes(hot_t[slice_of], 1, 2)
    hot = [hot_t[: gx // 2, :h], hot_t[gx // 2:, :h], hot_t[: gx // 2, h:], hot_t[gx // 2:, h:]]

    own_cnt = count(meta[None], slice_of * hot_slice, hot_slice, lambda s, p, o: (0, s, 0, 0))
    all_cnt = count(
        meta_flat, jnp.full((devices,), 0, i32) + me_x * hot_slice, hot_slice, lambda s, p, o: (p, s, 0, 0)
    )
    own_cnt = own_cnt.reshape(steps, 2, gx // 2, 1, hot_slice)
    all_cnt = all_cnt.reshape(steps, 2, devices // 2, 1, hot_slice)

    denom = 1.0 + bag_len.astype(f32)
    base = []
    source = in_t
    for s in range(steps):
        a0, a1, b0, b1 = base_sums(source, meta_all, in_base, s)
        base.append(jnp.concatenate([tree.reduce(a0, a1, True), tree.reduce(b0, b1, False)], axis=0))
        if devices > 64:
            source, base[s] = lax.optimization_barrier((source, base[s]))
    context = fetch_contexts(tree, me, out_table, meta_flat, context_owner[:, :, 0], cap)
    context = [jnp.pad(context[s].T, spare) for s in range(steps)]
    pairs = {(s, e): couple(own, meta_all, s, e) for s in range(steps) for e in range(s)}

    if devices > 64:
        base, context = lax.optimization_barrier((base, context))
    real = jnp.arange(feats)[:, None] < width
    for s in range(steps):
        centre = jnp.where(real, base[s] / denom[s][None, :], 0.0)
        c = tree.gather(centre[:h], centre[h:])
        g = own_grads(width, scale, centre, context[s], denom[s][None, :], own_cnt[s:s + 1], hot)
        g = tree.gather(g[:h], g[h:])
        new_a, new_b = hot_update(scale, all_cnt[s:s + 1], hot, c)
        hot = tree.gather_gx(new_a, new_b)
        for later in range(s + 1, steps):
            centre_add, context_add = absorb(width, g, c, *pairs[(later, s)])
            base[later] = base[later] - centre_add
            context[later] = context[later] - context_add
        in_t = update(in_t, meta_all, in_base, s, g)
        out_t = update(out_t, meta_all, out_base, s, g, c)
        if devices > 64:
            in_t, out_t, hot, base, context = lax.optimization_barrier((in_t, out_t, hot, base, context))

    hot = jnp.concatenate([jnp.concatenate(hot[:2], axis=0), jnp.concatenate(hot[2:], axis=0)], axis=1)
    place = me_x ^ jnp.arange(gx, dtype=i32)
    hot = hot[place // 2 + (gx // 2) * (place % 2)]
    hot = jnp.swapaxes(hot, 1, 2).reshape(hot_rows, feats)[:, :width]
    return in_t[:width].T, out_t[:width].T, hot


def solution(mesh):
    placed = (
        P(axes, None),
        P(axes, None),
        P(),
        P(None, axes, None),
        P(None, axes),
        P(None, axes, None),
        P(None, axes, None),
        P(None, axes),
        P(None, axes, None),
        P(None, axes),
        P(None, axes),
    )
    return jax.shard_map(
        body,
        mesh=mesh,
        in_specs=placed,
        out_specs=(P(axes, None), P(axes, None), P()),
        check_vma=False,
    )
```

```python
import functools
import jax
import jax.numpy as jnp
from jax import lax
from jax.experimental import pallas as pl
from jax.experimental.pallas import tpu as pltpu
from jax.sharding import PartitionSpec as P

learn_rate = 2.0
exact = lax.Precision.HIGHEST
axes = ("gx", "gy")
LANES = 128
SLOTS = 8
META = SLOTS + 16
GROUP = 4
f32, bf16, i32 = jnp.float32, jnp.bfloat16, jnp.int32
NN = (((1,), (0,)), ((), ()))
NT = (((1,), (1,)), ((), ()))
TN = (((0,), (0,)), ((), ()))


def swap(x, bit, devices):
    return lax.ppermute(x, axes, [(d, d ^ bit) for d in range(devices)])


def split3(x):
    hi = x.astype(bf16)
    rest = x - hi.astype(f32)
    mid = rest.astype(bf16)
    return hi, mid, (rest - mid.astype(f32)).astype(bf16)


def split2(x):
    hi = x.astype(bf16)
    return hi, (x - hi.astype(f32)).astype(bf16)


class Tree:
    def __init__(self, gx, gy):
        self.gx, self.gy = gx, gy
        self.devices = gx * gy
        self.low = [1 << b for b in range(gy.bit_length() - 1)]
        self.high = [gy << b for b in range(1, gx.bit_length() - 1)]
        self.core = gy

    def widen(self, x, bits, descending):
        m = len(bits)
        x = x.reshape((1,) * m + x.shape)
        order = list(range(m))
        if descending:
            order.reverse()
        for b in order:
            x = jnp.concatenate([x, swap(x, bits[b], self.devices)], axis=m - 1 - b)
        return x.reshape((-1,) + x.shape[m + 1:])

    def gather(self, a, b):
        out = []
        for part, descending in ((a, False), (b, True)):
            x = self.widen(part[None], self.low, False)
            x = self.widen(x, self.high, descending)
            out += [x, swap(x, self.core, self.devices)]
        return out

    def gather_gx(self, a, b):
        out = []
        for part, descending in ((a, False), (b, True)):
            x = self.widen(part[None], self.high, descending)
            out += [x, swap(x, self.core, self.devices)]
        return out

    def gather_one(self, x):
        x = self.widen(x[None], self.low, False)
        x = self.widen(x, self.high, False)
        return jnp.concatenate([x, swap(x, self.core, self.devices)], axis=0)

    def reduce(self, keep, send, descending):
        x = keep + swap(send, self.core, self.devices)
        m = len(self.high)
        x = x.reshape((2,) * m + (self.gy,) + x.shape[1:])
        order = list(range(m))
        if descending:
            order.reverse()
        for b in order:
            axis = m - 1 - b
            near = lax.slice_in_dim(x, 0, 1, axis=axis)
            far = lax.slice_in_dim(x, 1, 2, axis=axis)
            x = near + swap(far, self.high[b], self.devices)
        x = x.reshape(x.shape[m:])
        for bit in reversed(self.low):
            half = x.shape[0] // 2
            x = x[:half] + swap(x[half:], bit, self.devices)
        return x[0]

    def place_of(self, mask):
        bits = self.devices.bit_length() - 1
        g, low = mask // self.gy, mask % self.gy
        return (g % 2) * (1 << (bits - 1)) + (g // 2) * self.gy + low

    def slice_mask(self, place):
        half = self.gx // 2
        return place // half + 2 * (place % half)


def params(*semantics):
    return pltpu.CompilerParams(dimension_semantics=semantics, vmem_limit_bytes=40 * 2**20)


def cost(flops, nbytes, trans=0):
    return pl.CostEstimate(flops=int(flops), bytes_accessed=int(nbytes), transcendentals=int(trans))


def after(x, *earlier):
    return lax.optimization_barrier((x, earlier))[0]


def count_kernel(ids_ref, out_ref):
    groups = out_ref.shape[1]
    for s in range(out_ref.shape[0]):
        ids = ids_ref[s:s + 1, :]
        n = ids.shape[1]
        high = jnp.where(lax.broadcasted_iota(i32, (groups, n), 0) == ids // LANES, 1.0, 0.0)
        low = jnp.where(lax.broadcasted_iota(i32, (LANES, n), 0) == ids % LANES, 1.0, 0.0)
        total = lax.dot_general(high.astype(bf16), low.astype(bf16), NT, preferred_element_type=f32)
        out_ref[s] = total.astype(i32)


def count(ids, hot_rows):
    return pl.pallas_call(
        count_kernel,
        out_shape=jax.ShapeDtypeStruct((ids.shape[0], hot_rows // LANES, LANES), i32),
        compiler_params=pltpu.CompilerParams(vmem_limit_bytes=40 * 2**20),
        cost_estimate=cost(1e6, 1e5),
        name="count",
    )(ids)


def count_row(rows_ref, slice_at, width):
    at = SLOTS + slice_at * (width // LANES)
    rows = [rows_ref[pl.ds(at + q, 1), :] for q in range(width // LANES)]
    return jnp.concatenate(rows, axis=1).astype(f32)


def couple_kernel(own_ref, other_ref, in_ref, out_ref, wide):
    @pl.when(pl.program_id(0) == 0)
    def _():
        for k in range(SLOTS):
            wide[k] = jnp.broadcast_to(own_ref[0, :, k:k + 1], wide.shape[1:])

    for c in range(2):
        total = jnp.zeros(wide.shape[1:], f32)
        for k in range(SLOTS - 1):
            row = other_ref[c, 0, 0, k:k + 1, :]
            in_bag = wide[1] == row
            for j in range(2, SLOTS - 1):
                in_bag = in_bag | (wide[j] == row)
            total = total + jnp.where(in_bag, 1.0, 0.0) + jnp.where(wide[0] == row, 1.0, 0.0)
        in_ref[c, 0] = total.astype(bf16)
        same = wide[SLOTS - 1] == other_ref[c, 0, 0, SLOTS - 1:SLOTS, :]
        out_ref[c, 0] = jnp.where(same, 1.0, 0.0).astype(bf16)


def couple(own, meta, later, earlier):
    half, n = meta.shape[1], own.shape[1]
    shape = jax.ShapeDtypeStruct((2, half, n, n), bf16)
    spec = pl.BlockSpec((2, 1, n, n), lambda p: (0, p, 0, 0))
    return pl.pallas_call(
        couple_kernel,
        out_shape=(shape, shape),
        grid=(half,),
        in_specs=[
            pl.BlockSpec((1, n, SLOTS), lambda p: (later, 0, 0)),
            pl.BlockSpec((2, 1, 1, META, LANES), lambda p: (0, p, earlier, 0, 0)),
        ],
        out_specs=(spec, spec),
        scratch_shapes=[pltpu.VMEM((SLOTS, n, n), i32)],
        compiler_params=params("arbitrary"),
        cost_estimate=cost(half * 2 * n * n * 150, half * n * n * 8),
        name="couple",
    )(own, meta)


def local_rows(ids, rows, context):
    if context:
        return [ids[SLOTS - 1:SLOTS, :]]
    ids = jnp.where((ids >= 0) & (ids < rows), ids, -1)
    return [ids[0:1, :], jnp.max(ids[1:SLOTS - 1, :], axis=0, keepdims=True)]


def base_kernel(rows, base_ref, meta_ref, table_ref, a0, a1, b0, b1, parts):
    feats = table_ref.shape[0]

    @pl.when(pl.program_id(0) == 0)
    def _():
        for k, part in enumerate(split3(table_ref[...])):
            parts[k * feats:(k + 1) * feats, :] = part

    h = a0.shape[1]
    iota = lax.broadcasted_iota(i32, (rows, LANES), 0)
    for p in range(a0.shape[0]):
        picks = []
        for c in range(2):
            one, two = local_rows(meta_ref[c, p, 0, :SLOTS, :] - base_ref[0], rows, False)
            picks.append(jnp.where(iota == one, 1.0, 0.0) + jnp.where(iota == two, 1.0, 0.0))
        pick = jnp.concatenate(picks, axis=1).astype(bf16)
        total = jnp.dot(parts[...], pick, preferred_element_type=f32)
        total = total[:feats] + total[feats:2 * feats] + total[2 * feats:]
        a0[p] = total[:h, :LANES]
        a1[p] = total[:h, LANES:]
        b0[p] = total[h:, :LANES]
        b1[p] = total[h:, LANES:]


def base_sums(table_t, meta, base, step):
    half = meta.shape[1]
    feats, rows = table_t.shape
    shape = jax.ShapeDtypeStruct((half, feats // 2, LANES), f32)
    spec = pl.BlockSpec((GROUP, feats // 2, LANES), lambda p, b: (p, 0, 0))
    return pl.pallas_call(
        functools.partial(base_kernel, rows),
        out_shape=(shape,) * 4,
        grid_spec=pltpu.PrefetchScalarGridSpec(
            num_scalar_prefetch=1,
            grid=(half // GROUP,),
            in_specs=[
                pl.BlockSpec((2, GROUP, 1, META, LANES), lambda p, b: (0, p, step, 0, 0)),
                pl.BlockSpec((feats, rows), lambda p, b: (0, 0)),
            ],
            out_specs=(spec,) * 4,
            scratch_shapes=[pltpu.VMEM((3 * feats, rows), bf16)],
        ),
        compiler_params=params("arbitrary"),
        cost_estimate=cost(2 * 3 * half * 256 * feats * rows, half * 2 * feats * 512 + feats * rows * 4),
        name="base_sums",
    )(base, meta, table_t)


def tokens_of(r0, r1):
    return jnp.concatenate([r[p] for p in range(r0.shape[0]) for r in (r0, r1)], axis=1)


def update_kernel(rows, width, base_ref, meta_ref, table_ref, *refs):
    pick, out_ref = refs[-1], refs[-2]
    ga0, ga1, gb0, gb1 = refs[:4]
    context = len(refs) == 8

    @pl.when(pl.program_id(0) == 0)
    def _():
        out_ref[...] = table_ref[...]

    iota = lax.broadcasted_iota(i32, (LANES, rows), 1)
    for p in range(ga0.shape[0]):
        for c in range(2):
            ids = meta_ref[c, p, 0, :SLOTS, :] - base_ref[0]
            found = local_rows(ids, rows, context)
            found = jnp.concatenate(found + [found[0]] * (SLOTS - len(found)), axis=0).T
            hits = jnp.where(iota == found[:, 0:1], 1.0, 0.0)
            if not context:
                hits = hits + jnp.where(iota == found[:, 1:2], 1.0, 0.0)
            at = (2 * p + c) * LANES
            pick[at:at + LANES, :] = hits.astype(bf16)
    ga, gb = tokens_of(ga0, ga1), tokens_of(gb0, gb1)
    if context:
        pos0, pos1 = refs[4], refs[5]
        row = width - gb.shape[0]
        pos = jnp.concatenate(
            [r[p, row:row + 1, :] for p in range(pos0.shape[0]) for r in (pos0, pos1)], axis=1
        )
        ga, gb = ga * pos, gb * pos
    grad = jnp.concatenate([ga, gb], axis=0) * learn_rate
    feats = grad.shape[0]
    both = jnp.concatenate(split2(grad), axis=0)
    total = jnp.dot(both, pick[...], preferred_element_type=f32)
    out_ref[...] = out_ref[...] - (total[:feats] + total[feats:])


def update(table_t, meta, base, step, width, g, pos=()):
    half = meta.shape[1]
    feats, rows = table_t.shape
    piece = pl.BlockSpec((GROUP, feats // 2, LANES), lambda p, b: (p, 0, 0))
    whole = pl.BlockSpec((feats, rows), lambda p, b: (0, 0))
    arrays = list(g) + list(pos)
    return pl.pallas_call(
        functools.partial(update_kernel, rows, width),
        out_shape=jax.ShapeDtypeStruct((feats, rows), f32),
        grid_spec=pltpu.PrefetchScalarGridSpec(
            num_scalar_prefetch=1,
            grid=(half // GROUP,),
            in_specs=[pl.BlockSpec((2, GROUP, 1, META, LANES), lambda p, b: (0, p, step, 0, 0)), whole]
            + [piece] * len(arrays),
            out_specs=whole,
            scratch_shapes=[pltpu.VMEM((GROUP * 2 * LANES, rows), bf16)],
        ),
        compiler_params=params("arbitrary"),
        cost_estimate=cost(2 * 2 * half * 256 * feats * rows, half * 2 * feats * 512 * len(arrays) // 4),
        name="context_update" if pos else "update",
    )(base, meta, table_t, *arrays)


def absorb_kernel(width, ga0, ga1, gb0, gb1, ca0, ca1, cb0, cb1, in_ref, ctx_ref, c_out, x_out):
    @pl.when(pl.program_id(0) == 0)
    def _():
        c_out[...] = jnp.zeros_like(c_out)
        x_out[...] = jnp.zeros_like(x_out)

    group = ga0.shape[0]
    ga, gb = tokens_of(ga0, ga1), tokens_of(gb0, gb1)
    row = width - gb.shape[0]
    pos = gb[row:row + 1, :]
    grad = jnp.concatenate([ga, gb], axis=0)
    centre = jnp.concatenate([tokens_of(ca0, ca1), tokens_of(cb0, cb1)], axis=0) * pos
    feats = grad.shape[0]
    for value, ref, out in ((grad, in_ref, c_out), (centre, ctx_ref, x_out)):
        pairs = jnp.concatenate([ref[c, p] for p in range(group) for c in range(2)], axis=1)
        parts = jnp.concatenate(split3(value * learn_rate), axis=0)
        total = lax.dot_general(parts, pairs, NT, preferred_element_type=f32)
        out[...] += total[:feats] + total[feats:2 * feats] + total[2 * feats:]


def absorb(width, g, c, in_pairs, ctx_pairs):
    half, feats_half, n = g[0].shape
    piece = pl.BlockSpec((GROUP, feats_half, n), lambda p: (p, 0, 0))
    pair = pl.BlockSpec((2, GROUP, n, n), lambda p: (0, p, 0, 0))
    shape = jax.ShapeDtypeStruct((2 * feats_half, n), f32)
    spec = pl.BlockSpec((2 * feats_half, n), lambda p: (0, 0))
    return pl.pallas_call(
        functools.partial(absorb_kernel, width),
        out_shape=(shape, shape),
        grid=(half // GROUP,),
        in_specs=[piece] * 8 + [pair] * 2,
        out_specs=(spec, spec),
        compiler_params=params("arbitrary"),
        cost_estimate=cost(2 * 2 * 3 * half * 256 * feats_half * 2 * n, half * 256 * feats_half * 16),
        name="absorb",
    )(*g, *c, in_pairs, ctx_pairs)


def dot6(left, right, dims):
    m = left[0].shape[0]
    one = lax.dot_general(jnp.concatenate(left, axis=0), right[0], dims, preferred_element_type=f32)
    two = lax.dot_general(jnp.concatenate(left[:2], axis=0), right[1], dims, preferred_element_type=f32)
    three = lax.dot_general(left[0], right[2], dims, preferred_element_type=f32)
    return one[:m] + (one[m:2 * m] + two[:m]) + ((one[2 * m:] + two[m:]) + three)


def own_kernel(width, scale, slice_ref, c_ref, x_ref, denom_ref, meta_ref, a0, a1, b0, b1, out_ref, total):
    p = pl.program_id(0)

    @pl.when(p == 0)
    def _():
        total[...] = jnp.zeros_like(total)

    centre = c_ref[...]
    group, hot_slice = a0.shape[0], a0.shape[2]
    hot = jnp.concatenate([tokens_of(a0, a1), tokens_of(b0, b1)], axis=0)
    half = pl.num_programs(0) * group
    counts = [
        count_row(meta_ref.at[0], slice_ref[c * half + p * group + q], hot_slice)
        for q in range(group)
        for c in range(2)
    ]
    counts = jnp.concatenate(counts, axis=1)
    parts = split3(hot)
    scores = dot6(split3(centre.T), parts, NN)
    grad = (scale * counts) * jax.nn.sigmoid(scores)
    total[...] += dot6(parts, split3(grad), NT)

    @pl.when(p == pl.num_programs(0) - 1)
    def _():
        context = x_ref[...]
        positive = jnp.sum(centre * context, axis=0, keepdims=True)
        pos = jax.nn.sigmoid(positive) - 1.0
        grad = (pos * context + total[...]) / denom_ref[...]
        feature = lax.broadcasted_iota(i32, grad.shape, 0)
        out_ref[...] = jnp.where(feature == width, pos, grad)


def own_grads(width, scale, centre, context, denom, slice_of, meta, step, hot):
    feats, n = centre.shape
    half, feats_half, hot_slice = hot[0].shape
    group = max(1, 512 // hot_slice)
    whole = pl.BlockSpec((feats, n), lambda p, o: (0, 0))
    piece = pl.BlockSpec((group, feats_half, hot_slice), lambda p, o: (p, 0, 0))
    return pl.pallas_call(
        functools.partial(own_kernel, width, scale),
        out_shape=jax.ShapeDtypeStruct((feats, n), f32),
        grid_spec=pltpu.PrefetchScalarGridSpec(
            num_scalar_prefetch=1,
            grid=(half // group,),
            in_specs=[
                whole,
                whole,
                pl.BlockSpec((1, n), lambda p, o: (0, 0)),
                pl.BlockSpec((1, META, LANES), lambda p, o: (step, 0, 0)),
            ]
            + [piece] * 4,
            out_specs=whole,
            scratch_shapes=[pltpu.VMEM((feats, n), f32)],
        ),
        compiler_params=params("arbitrary"),
        cost_estimate=cost(2 * 2 * 6 * half * 2 * hot_slice * feats * n, half * 4 * feats_half * hot_slice * 4),
        name="own_grads",
    )(slice_of, centre, context, denom, meta, *hot)


def hot_kernel(scale, slice_ref, meta_ref, hot_a, hot_b, a0, a1, b0, b1, out_a, out_b, total, parts):
    p = pl.program_id(0)

    @pl.when(p == 0)
    def _():
        total[...] = jnp.zeros_like(total)
        hot = jnp.concatenate([hot_a[0], hot_b[0]], axis=0)
        for k, part in enumerate(split3(hot)):
            parts[k] = part

    group, n = a0.shape[0], a0.shape[2]
    hot_slice = hot_a.shape[2]
    centre = jnp.concatenate([tokens_of(a0, a1), tokens_of(b0, b1)], axis=0)
    scores = dot6(split3(centre.T), [parts[0], parts[1], parts[2]], NN)
    sums = []
    for q in range(group):
        grads = []
        for c in range(2):
            at = (2 * q + c) * n
            counts = count_row(meta_ref.at[c, q, 0], slice_ref[0], hot_slice)
            grads.append((scale * counts) * jax.nn.sigmoid(scores[at:at + n]))
        at = 2 * q * n
        sums.append(dot6(split3(centre[:, at:at + 2 * n]), split3(jnp.concatenate(grads, axis=0)), NN))
    while len(sums) > 1:
        sums = [a + b for a, b in zip(sums[::2], sums[1::2])]
    total[...] += sums[0]

    @pl.when(p == pl.num_programs(0) - 1)
    def _():
        h = out_a.shape[0]
        out_a[...] = hot_a[0] - learn_rate * total[:h, :]
        out_b[...] = hot_b[0] - learn_rate * total[h:, :]


def hot_update(scale, me_x, meta, step, hot, c):
    half, feats_half, n = c[0].shape
    hot_slice = hot[0].shape[2]
    shape = jax.ShapeDtypeStruct((feats_half, hot_slice), f32)
    out = pl.BlockSpec((feats_half, hot_slice), lambda p, o: (0, 0))
    first = pl.BlockSpec((1, feats_half, hot_slice), lambda p, o: (0, 0, 0))
    piece = pl.BlockSpec((GROUP, feats_half, n), lambda p, o: (p, 0, 0))
    return pl.pallas_call(
        functools.partial(hot_kernel, scale),
        out_shape=(shape, shape),
        grid_spec=pltpu.PrefetchScalarGridSpec(
            num_scalar_prefetch=1,
            grid=(half // GROUP,),
            in_specs=[
                pl.BlockSpec((2, GROUP, 1, META, LANES), lambda p, o: (0, p, step, 0, 0)),
                first,
                first,
            ]
            + [piece] * 4,
            out_specs=(out, out),
            scratch_shapes=[
                pltpu.VMEM((2 * feats_half, hot_slice), f32),
                pltpu.VMEM((3, 2 * feats_half, hot_slice), bf16),
            ],
        ),
        compiler_params=params("arbitrary"),
        cost_estimate=cost(2 * 2 * 6 * half * 256 * hot_slice * feats_half * 2, half * 256 * feats_half * 8),
        name="hot_update",
    )(me_x, meta, hot[0], hot[2], *c)


def fetch_contexts(tree, me, out_table, ids, owner, cap):
    rows, width = out_table.shape
    devices, steps, n = ids.shape
    ids = ids - me * rows
    mine = (ids >= 0) & (ids < rows)
    before = jnp.triu(jnp.ones((n, n), bf16), 1)
    rank = jnp.dot(mine.astype(bf16), before, preferred_element_type=f32).astype(i32)
    slots = jnp.arange(cap, dtype=i32)
    hit = mine[:, :, None, :] & (rank[:, :, None, :] == slots[None, None, :, None])
    wanted = jnp.sum(jnp.where(hit, ids[:, :, None, :], 0), axis=3)
    order = tree.place_of(me ^ jnp.arange(devices, dtype=i32))
    wanted = wanted[order].reshape(devices, steps * cap)
    got = lax.all_to_all(out_table[wanted], axes, split_axis=0, concat_axis=0, tiled=True)
    same = (owner[:, :, None] == owner[:, None, :]) & (
        jnp.arange(n)[None, :, None] > jnp.arange(n)[None, None, :]
    )
    own_rank = jnp.sum(same.astype(i32), axis=2)
    at = (owner * steps + jnp.arange(steps, dtype=i32)[:, None]) * cap + own_rank
    return got.reshape(devices * steps * cap, width)[at]


def body(
    in_table,
    out_table,
    hot_table,
    centre_owner,
    centre_row,
    bag_owner,
    bag_row,
    bag_len,
    context_owner,
    context_row,
    negative_ids,
):
    gx, gy = lax.axis_size("gx"), lax.axis_size("gy")
    tree = Tree(gx, gy)
    devices = tree.devices
    me_x = lax.axis_index("gx").astype(i32)
    me = me_x * gy + lax.axis_index("gy").astype(i32)
    steps, n, bag = bag_row.shape
    rows, width = in_table.shape
    out_rows = out_table.shape[0]
    hot_rows = hot_table.shape[0]
    neg = negative_ids.shape[1]
    cap = max(2, 2 * n // devices)
    hot_slice = hot_rows // gx
    feats = -(-(width + 1) // 16) * 16
    h = feats // 2
    scale = 16.0 / neg

    kept = jnp.arange(bag, dtype=i32)[None, None, :] < bag_len[:, :, None]
    centre_ids = centre_owner * rows + centre_row[:, :, None]
    bag_ids = bag_owner * rows + bag_row
    context_ids = context_owner * out_rows + context_row[:, :, None]
    own = jnp.concatenate([centre_ids, jnp.where(kept, bag_ids, -2), context_ids], axis=2)
    sent = jnp.concatenate([centre_ids, jnp.where(kept, bag_ids, -1), context_ids], axis=2)
    meta = jnp.concatenate([jnp.swapaxes(sent, 1, 2), count(negative_ids, hot_rows)], axis=1)
    meta_flat = tree.gather_one(meta.reshape(steps * META, LANES)).reshape(devices, steps, META, LANES)
    meta_all = meta_flat.reshape(2, devices // 2, steps, META, LANES)

    in_base = (me * rows).reshape(1)
    out_base = (me * out_rows).reshape(1)
    spare = ((0, feats - width), (0, 0))
    in_t = jnp.pad(in_table.T, spare)
    out_t = jnp.pad(out_table.T, spare)
    slice_of = me_x ^ tree.slice_mask(jnp.arange(gx, dtype=i32))
    hot_t = jnp.pad(hot_table, ((0, 0), (0, feats - width))).reshape(gx, hot_slice, feats)
    hot_t = jnp.swapaxes(hot_t[slice_of], 1, 2)
    hot = [hot_t[: gx // 2, :h], hot_t[gx // 2:, :h], hot_t[: gx // 2, h:], hot_t[gx // 2:, h:]]

    denom = 1.0 + bag_len.astype(f32)
    context_all = meta_flat[:, :, SLOTS - 1, :]
    owner = context_owner[:, :, 0]

    def base_of(s, table):
        a0, a1, b0, b1 = base_sums(table, meta_all, in_base, s)
        return jnp.concatenate([tree.reduce(a0, a1, True), tree.reduce(b0, b1, False)], axis=0)

    def contexts_of(first, last, table):
        got = fetch_contexts(tree, me, table, context_all[:, first:last], owner[first:last], cap)
        return [jnp.pad(got[k].T, spare) for k in range(last - first)]

    small = devices > 64
    base = [base_of(0, in_t)] + [None] * (steps - 1)
    context = contexts_of(0, 1, out_table)
    base_source = in_t
    real = jnp.arange(feats)[:, None] < width
    held = []
    added = [[] for _ in range(steps)]
    for s in range(steps):
        centre = jnp.where(real, base[s] / denom[s][None, :], 0.0)
        c = tree.gather(centre[:h], centre[h:])
        g = own_grads(width, scale, centre, context[s], denom[s][None, :], slice_of, meta, s, hot)
        g = tree.gather(g[:h], g[h:])
        if s == 0:
            context += contexts_of(1, steps, after(out_table, base[0], context[0]))
        if s + 1 < steps:
            base[s + 1] = base_of(s + 1, after(base_source, g if small else base[s]))
        due = [(later, s) for later in range(s + 1, steps)] if small else [(s + 1, e) for e in range(s + 1)]
        due = [] if s + 1 == steps else due
        pairs = [couple(after(own, base[s]), meta_all, later, e) for later, e in due]
        if s > 0:
            c[0], in_t, out_t = lax.optimization_barrier((c[0], in_t, out_t))
        new_a, new_b = hot_update(scale, me_x.reshape(1), meta_all, s, hot, c)
        hot = tree.gather_gx(new_a, new_b)
        held.append((g, c))
        for (later, e), pair in zip(due, pairs):
            added[later].append(absorb(width, *held[e], *pair))
        in_t = update(in_t, meta_all, in_base, s, width, g)
        out_t = update(out_t, meta_all, out_base, s, width, c, g[2:])
        if s + 1 < steps:
            for centre_add, context_add in added[s + 1]:
                base[s + 1] = base[s + 1] - centre_add
                context[s + 1] = context[s + 1] - context_add
            if small:
                in_t, out_t, hot, base, context, added = lax.optimization_barrier(
                    (in_t, out_t, hot, base, context, added)
                )

    hot = jnp.concatenate([jnp.concatenate(hot[:2], axis=0), jnp.concatenate(hot[2:], axis=0)], axis=1)
    place = me_x ^ jnp.arange(gx, dtype=i32)
    hot = hot[place // 2 + (gx // 2) * (place % 2)]
    hot = jnp.swapaxes(hot, 1, 2).reshape(hot_rows, feats)[:, :width]
    return in_t[:width].T, out_t[:width].T, hot


def solution(mesh):
    placed = (
        P(axes, None),
        P(axes, None),
        P(),
        P(None, axes, None),
        P(None, axes),
        P(None, axes, None),
        P(None, axes, None),
        P(None, axes),
        P(None, axes, None),
        P(None, axes),
        P(None, axes),
    )
    return jax.shard_map(
        body,
        mesh=mesh,
        in_specs=placed,
        out_specs=(P(axes, None), P(axes, None), P()),
        check_vma=False,
    )
```

```python
import functools
import jax
import jax.numpy as jnp
from jax import lax
from jax.experimental import pallas as pl
from jax.experimental.pallas import tpu as pltpu
from jax.sharding import PartitionSpec as P

learn_rate = 2.0
exact = lax.Precision.HIGHEST
axes = ("gx", "gy")
LANES = 128
SLOTS = 8
META = SLOTS + 16
GROUP = 4
f32, bf16, i32 = jnp.float32, jnp.bfloat16, jnp.int32
NN = (((1,), (0,)), ((), ()))
NT = (((1,), (1,)), ((), ()))
TN = (((0,), (0,)), ((), ()))


def swap(x, bit, devices):
    return lax.ppermute(x, axes, [(d, d ^ bit) for d in range(devices)])


def split3(x):
    hi = x.astype(bf16)
    rest = x - hi.astype(f32)
    mid = rest.astype(bf16)
    return hi, mid, (rest - mid.astype(f32)).astype(bf16)


def split2(x):
    hi = x.astype(bf16)
    return hi, (x - hi.astype(f32)).astype(bf16)


class Tree:
    def __init__(self, gx, gy):
        self.gx, self.gy = gx, gy
        self.devices = gx * gy
        self.low = [1 << b for b in range(gy.bit_length() - 1)]
        self.high = [gy << b for b in range(1, gx.bit_length() - 1)]
        self.core = gy

    def widen(self, parts, plans):
        m = len(plans[0])
        tails = [p.shape for p in parts]
        parts = [p.reshape((1,) * m + p.shape) for p in parts]
        for k in range(m):
            got = yield parts, [swap(p, plan[k][0], self.devices) for p, plan in zip(parts, plans)]
            parts = [jnp.concatenate([p, g], axis=plan[k][1]) for p, g, plan in zip(parts, got, plans)]
        return [p.reshape((-1,) + t) for p, t in zip(parts, tails)]

    def plans(self, with_low):
        mh, ml = len(self.high), len(self.low) if with_low else 0
        low = [(self.low[b], mh + ml - 1 - b) for b in reversed(range(ml))]
        high = [(self.high[b], mh - 1 - b) for b in range(mh)]
        return [low + high, low + high[::-1]]

    def gather(self, a, b, with_low=True):
        x, y = yield from self.widen([a, b], self.plans(with_low))
        got = yield [x, y], [swap(x, self.core, self.devices), swap(y, self.core, self.devices)]
        return [x, got[0], y, got[1]]

    def gather_one(self, x):
        (x,) = yield from self.widen([x], self.plans(True)[:1])
        got = yield [x], [swap(x, self.core, self.devices)]
        return jnp.concatenate([x, got[0]], axis=0)

    def reduce(self, a0, a1, b0, b1):
        got = yield [a1, b1], [swap(a1, self.core, self.devices), swap(b1, self.core, self.devices)]
        shape = (2,) * (len(self.high) + len(self.low)) + a0.shape[1:]
        parts = [(a0 + got[0]).reshape(shape), (b0 + got[1]).reshape(shape)]
        plans = [plan[::-1] for plan in self.plans(True)]
        for k in range(len(plans[0])):
            near = [lax.slice_in_dim(p, 0, 1, axis=plan[k][1]) for p, plan in zip(parts, plans)]
            far = [lax.slice_in_dim(p, 1, 2, axis=plan[k][1]) for p, plan in zip(parts, plans)]
            got = yield far, [swap(p, plan[k][0], self.devices) for p, plan in zip(far, plans)]
            parts = [p + g for p, g in zip(near, got)]
        return jnp.concatenate([p.reshape(p.shape[-2:]) for p in parts], axis=0)

    def place_of(self, mask):
        bits = self.devices.bit_length() - 1
        g, low = mask // self.gy, mask % self.gy
        return (g % 2) * (1 << (bits - 1)) + (g // 2) * self.gy + low

    def slice_mask(self, place):
        half = self.gx // 2
        return place // half + 2 * (place % half)


def params(*semantics):
    return pltpu.CompilerParams(dimension_semantics=semantics, vmem_limit_bytes=40 * 2**20)


def cost(flops, nbytes, trans=0):
    return pl.CostEstimate(flops=int(flops), bytes_accessed=int(nbytes), transcendentals=int(trans))


def after(x, *earlier):
    return lax.optimization_barrier((x, earlier))[0]


class Lane:
    def __init__(self, chain, stages):
        self.chain, self.left = chain, stages
        self.sent, self.got = next(chain)


def stage(lanes, fill=None):
    lanes = [lane for lane in lanes if lane is not None and lane.left > 0]
    sent = [lane.sent for lane in lanes]
    beside = fill(lambda x: after(x, sent)) if fill is not None else ()
    got, beside = lax.optimization_barrier(([lane.got for lane in lanes], beside))
    for lane, arrived in zip(lanes, got):
        lane.left -= 1
        try:
            lane.sent, lane.got = lane.chain.send(arrived)
        except StopIteration as end:
            lane.result = end.value
    return beside


def count_kernel(ids_ref, out_ref):
    groups = out_ref.shape[1]
    for s in range(out_ref.shape[0]):
        ids = ids_ref[s:s + 1, :]
        n = ids.shape[1]
        high = jnp.where(lax.broadcasted_iota(i32, (groups, n), 0) == ids // LANES, 1.0, 0.0)
        low = jnp.where(lax.broadcasted_iota(i32, (LANES, n), 0) == ids % LANES, 1.0, 0.0)
        total = lax.dot_general(high.astype(bf16), low.astype(bf16), NT, preferred_element_type=f32)
        out_ref[s] = total.astype(i32)


def count(ids, hot_rows):
    return pl.pallas_call(
        count_kernel,
        out_shape=jax.ShapeDtypeStruct((ids.shape[0], hot_rows // LANES, LANES), i32),
        compiler_params=pltpu.CompilerParams(vmem_limit_bytes=40 * 2**20),
        cost_estimate=cost(1e6, 1e5),
        name="count",
    )(ids)


def count_row(rows_ref, slice_at, width):
    at = SLOTS + slice_at * (width // LANES)
    rows = [rows_ref[pl.ds(at + q, 1), :] for q in range(width // LANES)]
    return jnp.concatenate(rows, axis=1).astype(f32)


def couple_kernel(own_ref, other_ref, in_ref, out_ref, wide):
    @pl.when(pl.program_id(0) == 0)
    def _():
        for k in range(SLOTS):
            wide[k] = jnp.broadcast_to(own_ref[0, :, k:k + 1], wide.shape[1:])

    for c in range(2):
        total = jnp.zeros(wide.shape[1:], f32)
        for k in range(SLOTS - 1):
            row = other_ref[c, 0, 0, k:k + 1, :]
            in_bag = wide[1] == row
            for j in range(2, SLOTS - 1):
                in_bag = in_bag | (wide[j] == row)
            total = total + jnp.where(in_bag, 1.0, 0.0) + jnp.where(wide[0] == row, 1.0, 0.0)
        in_ref[c, 0] = total.astype(bf16)
        same = wide[SLOTS - 1] == other_ref[c, 0, 0, SLOTS - 1:SLOTS, :]
        out_ref[c, 0] = jnp.where(same, 1.0, 0.0).astype(bf16)


def couple(own, meta, later, earlier):
    half, n = meta.shape[1], own.shape[1]
    shape = jax.ShapeDtypeStruct((2, half, n, n), bf16)
    spec = pl.BlockSpec((2, 1, n, n), lambda p: (0, p, 0, 0))
    return pl.pallas_call(
        couple_kernel,
        out_shape=(shape, shape),
        grid=(half,),
        in_specs=[
            pl.BlockSpec((1, n, SLOTS), lambda p: (later, 0, 0)),
            pl.BlockSpec((2, 1, 1, META, LANES), lambda p: (0, p, earlier, 0, 0)),
        ],
        out_specs=(spec, spec),
        scratch_shapes=[pltpu.VMEM((SLOTS, n, n), i32)],
        compiler_params=params("arbitrary"),
        cost_estimate=cost(half * 2 * n * n * 150, half * n * n * 8),
        name="couple",
    )(own, meta)


def local_rows(ids, rows, context):
    if context:
        return [ids[SLOTS - 1:SLOTS, :]]
    ids = jnp.where((ids >= 0) & (ids < rows), ids, -1)
    return [ids[0:1, :], jnp.max(ids[1:SLOTS - 1, :], axis=0, keepdims=True)]


def base_kernel(rows, base_ref, meta_ref, table_ref, a0, a1, b0, b1, parts):
    feats = table_ref.shape[0]

    @pl.when(pl.program_id(0) == 0)
    def _():
        for k, part in enumerate(split3(table_ref[...])):
            parts[k * feats:(k + 1) * feats, :] = part

    h = a0.shape[1]
    iota = lax.broadcasted_iota(i32, (rows, LANES), 0)
    for p in range(a0.shape[0]):
        picks = []
        for c in range(2):
            one, two = local_rows(meta_ref[c, p, 0, :SLOTS, :] - base_ref[0], rows, False)
            picks.append(jnp.where(iota == one, 1.0, 0.0) + jnp.where(iota == two, 1.0, 0.0))
        pick = jnp.concatenate(picks, axis=1).astype(bf16)
        total = jnp.dot(parts[...], pick, preferred_element_type=f32)
        total = total[:feats] + total[feats:2 * feats] + total[2 * feats:]
        a0[p] = total[:h, :LANES]
        a1[p] = total[:h, LANES:]
        b0[p] = total[h:, :LANES]
        b1[p] = total[h:, LANES:]


def base_sums(table_t, meta, base, step):
    half = meta.shape[1]
    feats, rows = table_t.shape
    shape = jax.ShapeDtypeStruct((half, feats // 2, LANES), f32)
    spec = pl.BlockSpec((GROUP, feats // 2, LANES), lambda p, b: (p, 0, 0))
    return pl.pallas_call(
        functools.partial(base_kernel, rows),
        out_shape=(shape,) * 4,
        grid_spec=pltpu.PrefetchScalarGridSpec(
            num_scalar_prefetch=1,
            grid=(half // GROUP,),
            in_specs=[
                pl.BlockSpec((2, GROUP, 1, META, LANES), lambda p, b: (0, p, step, 0, 0)),
                pl.BlockSpec((feats, rows), lambda p, b: (0, 0)),
            ],
            out_specs=(spec,) * 4,
            scratch_shapes=[pltpu.VMEM((3 * feats, rows), bf16)],
        ),
        compiler_params=params("arbitrary"),
        cost_estimate=cost(2 * 3 * half * 256 * feats * rows, half * 2 * feats * 512 + feats * rows * 4),
        name="base_sums",
    )(base, meta, table_t)


def tokens_of(r0, r1):
    return jnp.concatenate([r[p] for p in range(r0.shape[0]) for r in (r0, r1)], axis=1)


def update_kernel(rows, width, base_ref, meta_ref, table_ref, *refs):
    pick, out_ref = refs[-1], refs[-2]
    ga0, ga1, gb0, gb1 = refs[:4]
    context = len(refs) == 8

    @pl.when(pl.program_id(0) == 0)
    def _():
        out_ref[...] = table_ref[...]

    iota = lax.broadcasted_iota(i32, (LANES, rows), 1)
    for p in range(ga0.shape[0]):
        for c in range(2):
            ids = meta_ref[c, p, 0, :SLOTS, :] - base_ref[0]
            found = local_rows(ids, rows, context)
            found = jnp.concatenate(found + [found[0]] * (SLOTS - len(found)), axis=0).T
            hits = jnp.where(iota == found[:, 0:1], 1.0, 0.0)
            if not context:
                hits = hits + jnp.where(iota == found[:, 1:2], 1.0, 0.0)
            at = (2 * p + c) * LANES
            pick[at:at + LANES, :] = hits.astype(bf16)
    ga, gb = tokens_of(ga0, ga1), tokens_of(gb0, gb1)
    if context:
        pos0, pos1 = refs[4], refs[5]
        row = width - gb.shape[0]
        pos = jnp.concatenate(
            [r[p, row:row + 1, :] for p in range(pos0.shape[0]) for r in (pos0, pos1)], axis=1
        )
        ga, gb = ga * pos, gb * pos
    grad = jnp.concatenate([ga, gb], axis=0) * learn_rate
    feats = grad.shape[0]
    both = jnp.concatenate(split2(grad), axis=0)
    total = jnp.dot(both, pick[...], preferred_element_type=f32)
    out_ref[...] = out_ref[...] - (total[:feats] + total[feats:])


def update(table_t, meta, base, step, width, g, pos=()):
    half = meta.shape[1]
    feats, rows = table_t.shape
    piece = pl.BlockSpec((GROUP, feats // 2, LANES), lambda p, b: (p, 0, 0))
    whole = pl.BlockSpec((feats, rows), lambda p, b: (0, 0))
    arrays = list(g) + list(pos)
    return pl.pallas_call(
        functools.partial(update_kernel, rows, width),
        out_shape=jax.ShapeDtypeStruct((feats, rows), f32),
        grid_spec=pltpu.PrefetchScalarGridSpec(
            num_scalar_prefetch=1,
            grid=(half // GROUP,),
            in_specs=[pl.BlockSpec((2, GROUP, 1, META, LANES), lambda p, b: (0, p, step, 0, 0)), whole]
            + [piece] * len(arrays),
            out_specs=whole,
            scratch_shapes=[pltpu.VMEM((GROUP * 2 * LANES, rows), bf16)],
        ),
        compiler_params=params("arbitrary"),
        cost_estimate=cost(2 * 2 * half * 256 * feats * rows, half * 2 * feats * 512 * len(arrays) // 4),
        name="context_update" if pos else "update",
    )(base, meta, table_t, *arrays)


def absorb_kernel(width, ga0, ga1, gb0, gb1, ca0, ca1, cb0, cb1, in_ref, ctx_ref, c_out, x_out):
    @pl.when(pl.program_id(0) == 0)
    def _():
        c_out[...] = jnp.zeros_like(c_out)
        x_out[...] = jnp.zeros_like(x_out)

    group = ga0.shape[0]
    ga, gb = tokens_of(ga0, ga1), tokens_of(gb0, gb1)
    row = width - gb.shape[0]
    pos = gb[row:row + 1, :]
    grad = jnp.concatenate([ga, gb], axis=0)
    centre = jnp.concatenate([tokens_of(ca0, ca1), tokens_of(cb0, cb1)], axis=0) * pos
    feats = grad.shape[0]
    for value, ref, out in ((grad, in_ref, c_out), (centre, ctx_ref, x_out)):
        pairs = jnp.concatenate([ref[c, p] for p in range(group) for c in range(2)], axis=1)
        parts = jnp.concatenate(split3(value * learn_rate), axis=0)
        total = lax.dot_general(parts, pairs, NT, preferred_element_type=f32)
        out[...] += total[:feats] + total[feats:2 * feats] + total[2 * feats:]


def absorb(width, g, c, in_pairs, ctx_pairs):
    half, feats_half, n = g[0].shape
    piece = pl.BlockSpec((GROUP, feats_half, n), lambda p: (p, 0, 0))
    pair = pl.BlockSpec((2, GROUP, n, n), lambda p: (0, p, 0, 0))
    shape = jax.ShapeDtypeStruct((2 * feats_half, n), f32)
    spec = pl.BlockSpec((2 * feats_half, n), lambda p: (0, 0))
    return pl.pallas_call(
        functools.partial(absorb_kernel, width),
        out_shape=(shape, shape),
        grid=(half // GROUP,),
        in_specs=[piece] * 8 + [pair] * 2,
        out_specs=(spec, spec),
        compiler_params=params("arbitrary"),
        cost_estimate=cost(2 * 2 * 3 * half * 256 * feats_half * 2 * n, half * 256 * feats_half * 16),
        name="absorb",
    )(*g, *c, in_pairs, ctx_pairs)


def dot6(left, right, dims):
    m = left[0].shape[0]
    one = lax.dot_general(jnp.concatenate(left, axis=0), right[0], dims, preferred_element_type=f32)
    two = lax.dot_general(jnp.concatenate(left[:2], axis=0), right[1], dims, preferred_element_type=f32)
    three = lax.dot_general(left[0], right[2], dims, preferred_element_type=f32)
    return one[:m] + (one[m:2 * m] + two[:m]) + ((one[2 * m:] + two[m:]) + three)


def own_kernel(width, scale, slice_ref, c_ref, x_ref, denom_ref, meta_ref, a0, a1, b0, b1, out_ref, total):
    p = pl.program_id(0)

    @pl.when(p == 0)
    def _():
        total[...] = jnp.zeros_like(total)

    centre = c_ref[...]
    group, hot_slice = a0.shape[0], a0.shape[2]
    hot = jnp.concatenate([tokens_of(a0, a1), tokens_of(b0, b1)], axis=0)
    half = pl.num_programs(0) * group
    counts = [
        count_row(meta_ref.at[0], slice_ref[c * half + p * group + q], hot_slice)
        for q in range(group)
        for c in range(2)
    ]
    counts = jnp.concatenate(counts, axis=1)
    parts = split3(hot)
    scores = dot6(split3(centre.T), parts, NN)
    grad = (scale * counts) * jax.nn.sigmoid(scores)
    total[...] += dot6(parts, split3(grad), NT)

    @pl.when(p == pl.num_programs(0) - 1)
    def _():
        context = x_ref[...]
        positive = jnp.sum(centre * context, axis=0, keepdims=True)
        pos = jax.nn.sigmoid(positive) - 1.0
        grad = (pos * context + total[...]) / denom_ref[...]
        feature = lax.broadcasted_iota(i32, grad.shape, 0)
        out_ref[...] = jnp.where(feature == width, pos, grad)


def own_grads(width, scale, centre, context, denom, slice_of, meta, step, hot):
    feats, n = centre.shape
    half, feats_half, hot_slice = hot[0].shape
    group = max(1, 512 // hot_slice)
    whole = pl.BlockSpec((feats, n), lambda p, o: (0, 0))
    piece = pl.BlockSpec((group, feats_half, hot_slice), lambda p, o: (p, 0, 0))
    return pl.pallas_call(
        functools.partial(own_kernel, width, scale),
        out_shape=jax.ShapeDtypeStruct((feats, n), f32),
        grid_spec=pltpu.PrefetchScalarGridSpec(
            num_scalar_prefetch=1,
            grid=(half // group,),
            in_specs=[
                whole,
                whole,
                pl.BlockSpec((1, n), lambda p, o: (0, 0)),
                pl.BlockSpec((1, META, LANES), lambda p, o: (step, 0, 0)),
            ]
            + [piece] * 4,
            out_specs=whole,
            scratch_shapes=[pltpu.VMEM((feats, n), f32)],
        ),
        compiler_params=params("arbitrary"),
        cost_estimate=cost(2 * 2 * 6 * half * 2 * hot_slice * feats * n, half * 4 * feats_half * hot_slice * 4),
        name="own_grads",
    )(slice_of, centre, context, denom, meta, *hot)


def hot_kernel(scale, slice_ref, meta_ref, hot_a, hot_b, a0, a1, b0, b1, out_a, out_b, total, parts):
    p = pl.program_id(0)

    @pl.when(p == 0)
    def _():
        total[...] = jnp.zeros_like(total)
        hot = jnp.concatenate([hot_a[0], hot_b[0]], axis=0)
        for k, part in enumerate(split3(hot)):
            parts[k] = part

    group, n = a0.shape[0], a0.shape[2]
    hot_slice = hot_a.shape[2]
    centre = jnp.concatenate([tokens_of(a0, a1), tokens_of(b0, b1)], axis=0)
    scores = dot6(split3(centre.T), [parts[0], parts[1], parts[2]], NN)
    sums = []
    for q in range(group):
        grads = []
        for c in range(2):
            at = (2 * q + c) * n
            counts = count_row(meta_ref.at[c, q, 0], slice_ref[0], hot_slice)
            grads.append((scale * counts) * jax.nn.sigmoid(scores[at:at + n]))
        at = 2 * q * n
        sums.append(dot6(split3(centre[:, at:at + 2 * n]), split3(jnp.concatenate(grads, axis=0)), NN))
    while len(sums) > 1:
        sums = [a + b for a, b in zip(sums[::2], sums[1::2])]
    total[...] += sums[0]

    @pl.when(p == pl.num_programs(0) - 1)
    def _():
        h = out_a.shape[0]
        out_a[...] = hot_a[0] - learn_rate * total[:h, :]
        out_b[...] = hot_b[0] - learn_rate * total[h:, :]


def hot_update(scale, me_x, meta, step, hot, c):
    half, feats_half, n = c[0].shape
    hot_slice = hot[0].shape[2]
    shape = jax.ShapeDtypeStruct((feats_half, hot_slice), f32)
    out = pl.BlockSpec((feats_half, hot_slice), lambda p, o: (0, 0))
    first = pl.BlockSpec((1, feats_half, hot_slice), lambda p, o: (0, 0, 0))
    piece = pl.BlockSpec((GROUP, feats_half, n), lambda p, o: (p, 0, 0))
    return pl.pallas_call(
        functools.partial(hot_kernel, scale),
        out_shape=(shape, shape),
        grid_spec=pltpu.PrefetchScalarGridSpec(
            num_scalar_prefetch=1,
            grid=(half // GROUP,),
            in_specs=[
                pl.BlockSpec((2, GROUP, 1, META, LANES), lambda p, o: (0, p, step, 0, 0)),
                first,
                first,
            ]
            + [piece] * 4,
            out_specs=(out, out),
            scratch_shapes=[
                pltpu.VMEM((2 * feats_half, hot_slice), f32),
                pltpu.VMEM((3, 2 * feats_half, hot_slice), bf16),
            ],
        ),
        compiler_params=params("arbitrary"),
        cost_estimate=cost(2 * 2 * 6 * half * 256 * hot_slice * feats_half * 2, half * 256 * feats_half * 8),
        name="hot_update",
    )(me_x, meta, hot[0], hot[2], *c)


def fetch_contexts(tree, me, out_table, ids, owner, cap):
    rows, width = out_table.shape
    devices, steps, n = ids.shape
    ids = ids - me * rows
    mine = (ids >= 0) & (ids < rows)
    before = jnp.triu(jnp.ones((n, n), bf16), 1)
    rank = jnp.dot(mine.astype(bf16), before, preferred_element_type=f32).astype(i32)
    slots = jnp.arange(cap, dtype=i32)
    hit = mine[:, :, None, :] & (rank[:, :, None, :] == slots[None, None, :, None])
    wanted = jnp.sum(jnp.where(hit, ids[:, :, None, :], 0), axis=3)
    order = tree.place_of(me ^ jnp.arange(devices, dtype=i32))
    wanted = wanted[order].reshape(devices, steps * cap)
    got = lax.all_to_all(out_table[wanted], axes, split_axis=0, concat_axis=0, tiled=True)
    same = (owner[:, :, None] == owner[:, None, :]) & (
        jnp.arange(n)[None, :, None] > jnp.arange(n)[None, None, :]
    )
    own_rank = jnp.sum(same.astype(i32), axis=2)
    at = (owner * steps + jnp.arange(steps, dtype=i32)[:, None]) * cap + own_rank
    return got.reshape(devices * steps * cap, width)[at]


def body(
    in_table,
    out_table,
    hot_table,
    centre_owner,
    centre_row,
    bag_owner,
    bag_row,
    bag_len,
    context_owner,
    context_row,
    negative_ids,
):
    gx, gy = lax.axis_size("gx"), lax.axis_size("gy")
    tree = Tree(gx, gy)
    devices = tree.devices
    me_x = lax.axis_index("gx").astype(i32)
    me = me_x * gy + lax.axis_index("gy").astype(i32)
    steps, n, bag = bag_row.shape
    rows, width = in_table.shape
    out_rows = out_table.shape[0]
    hot_rows = hot_table.shape[0]
    neg = negative_ids.shape[1]
    cap = max(2, 2 * n // devices)
    hot_slice = hot_rows // gx
    feats = -(-(width + 1) // 16) * 16
    h = feats // 2
    scale = 16.0 / neg

    kept = jnp.arange(bag, dtype=i32)[None, None, :] < bag_len[:, :, None]
    centre_ids = centre_owner * rows + centre_row[:, :, None]
    bag_ids = bag_owner * rows + bag_row
    context_ids = context_owner * out_rows + context_row[:, :, None]
    own = jnp.concatenate([centre_ids, jnp.where(kept, bag_ids, -2), context_ids], axis=2)
    sent = jnp.concatenate([centre_ids, jnp.where(kept, bag_ids, -1), context_ids], axis=2)
    meta = jnp.concatenate([jnp.swapaxes(sent, 1, 2), count(negative_ids, hot_rows)], axis=1)
    span = len(tree.low) + len(tree.high) + 1
    short = len(tree.high) + 1
    lane = Lane(tree.gather_one(meta.reshape(steps * META, LANES)), span)
    while lane.left:
        stage([lane])
    meta_flat = lane.result.reshape(devices, steps, META, LANES)
    meta_all = meta_flat.reshape(2, devices // 2, steps, META, LANES)

    small = devices > 64
    in_base = (me * rows).reshape(1)
    out_base = (me * out_rows).reshape(1)
    spare = ((0, feats - width), (0, 0))
    in_t = jnp.pad(in_table.T, spare)
    source = in_t
    part = base_sums(source, meta_all, in_base, 0)
    hot_t, out_late = after((hot_table, out_table), part[0])
    out_t = jnp.pad(out_late.T, spare)
    slice_of = me_x ^ tree.slice_mask(jnp.arange(gx, dtype=i32))
    hot_t = jnp.pad(hot_t, ((0, 0), (0, feats - width))).reshape(gx, hot_slice, feats)
    hot_t = jnp.swapaxes(hot_t[slice_of], 1, 2)
    hot = [hot_t[: gx // 2, :h], hot_t[gx // 2:, :h], hot_t[: gx // 2, h:], hot_t[gx // 2:, h:]]
    denom = 1.0 + bag_len.astype(f32)
    got = fetch_contexts(tree, me, out_table, meta_flat[:, :, SLOTS - 1, :], context_owner[:, :, 0], cap)
    context = [jnp.pad(got[k].T, spare) for k in range(steps)]

    def sums(s):
        return lambda gate: base_sums(gate(source), meta_all, in_base, s)

    def pair(later, e):
        return lambda gate: couple(gate(own), meta_all, later, e)

    def run(lanes, fills, kept, until):
        while until.left:
            name, fill = fills.pop(0) if fills else (None, None)
            beside = stage(lanes, fill)
            if name is not None:
                kept[name] = beside

    kept = {}
    lane = Lane(tree.reduce(*part), span)
    fills = [] if small else [(None, None), (("sums", 1), sums(1)), (("pair", 1, 0), pair(1, 0))]
    run([lane], fills[: span] if steps > 1 else [], kept, lane)
    base = [lane.result] + [None] * (steps - 1)
    real = jnp.arange(feats)[:, None] < width
    held = []
    added = [[] for _ in range(steps)]
    tables = [in_t, out_t]

    def grow(s, which):
        def fill(gate):
            g, c = held[s]
            if which == 0:
                return update(gate(tables[0]), meta_all, in_base, s, width, g)
            return update(gate(tables[1]), meta_all, out_base, s, width, c, g[2:])

        return fill

    def soak(later, e):
        def fill(gate):
            g, c = held[e]
            return absorb(width, [gate(g[0])] + g[1:], c, *kept[("pair", later, e)])

        return fill

    for s in range(steps):
        last = s + 1 == steps
        centre = jnp.where(real, base[s] / denom[s][None, :], 0.0)
        c_lane = Lane(tree.gather(centre[:h], centre[h:]), span)
        g = stage(
            [c_lane],
            lambda gate: own_grads(
                width, scale, gate(centre), context[s], denom[s][None, :], slice_of, meta, s, hot
            ),
        )
        g_lane = Lane(tree.gather(g[:h], g[h:]), span)
        fills = []
        if not small:
            if s > 0:
                fills.append((("table", 1), grow(s - 1, 1)))
            for e in range(s + 1 if not last else 0):
                if ("pair", s + 1, e) not in kept:
                    fills.append((("pair", s + 1, e), pair(s + 1, e)))
            if s > 0:
                fills.append((("table", 0), grow(s - 1, 0)))
            if s + 2 < steps:
                fills.append((("sums", s + 2), sums(s + 2)))
                fills.append((("pair", s + 2, s), pair(s + 2, s)))
        r_lane = None
        while c_lane.left:
            if c_lane.left == 1 and not small and not last:
                if ("sums", s + 1) not in kept:
                    kept[("sums", s + 1)] = base_sums(source, meta_all, in_base, s + 1)
                r_lane = Lane(tree.reduce(*kept[("sums", s + 1)]), span)
            name, fill = fills.pop(0) if fills else (None, None)
            beside = stage([c_lane, g_lane, r_lane], fill)
            if name is not None:
                kept[name] = beside
        for name, fill in fills:
            kept[name] = fill(lambda x: x)
        for which in (0, 1):
            tables[which] = kept.pop(("table", which), tables[which])
        c = c_lane.result
        new_a, new_b = stage(
            [g_lane, r_lane],
            lambda gate: hot_update(scale, me_x.reshape(1), meta_all, s, hot, [gate(c[0])] + c[1:]),
        )
        while g_lane.left:
            stage([g_lane, r_lane])
        held.append((g_lane.result, c))
        h_lane = Lane(tree.gather(new_a, new_b, False), short)
        due = [(later, s) for later in range(s + 1, steps)] if small else [(s + 1, e) for e in range(s, -1, -1)]
        due = [] if last else due
        if small:
            for later, e in due:
                kept[("pair", later, e)] = couple(own, meta_all, later, e)
        fills = [(("soak", later, e), soak(later, e)) for later, e in due]
        if last or small:
            fills += [(("table", 1), grow(s, 1)), (("table", 0), grow(s, 0))]
        run([h_lane, r_lane], fills, kept, h_lane)
        for name, fill in fills:
            kept[name] = fill(lambda x: x)
        for which in (0, 1):
            tables[which] = kept.pop(("table", which), tables[which])
        for later, e in due:
            added[later].append(kept.pop(("soak", later, e)))
        hot = h_lane.result
        if not last:
            if small:
                source, tables, hot, context, added = lax.optimization_barrier(
                    (source, tables, hot, context, added)
                )
                r_lane = Lane(tree.reduce(*base_sums(source, meta_all, in_base, s + 1)), span)
            while r_lane.left:
                stage([r_lane])
            base[s + 1] = r_lane.result
            for centre_add, context_add in added[s + 1]:
                base[s + 1] = base[s + 1] - centre_add
                context[s + 1] = context[s + 1] - context_add
    in_t, out_t = tables

    hot = jnp.concatenate([jnp.concatenate(hot[:2], axis=0), jnp.concatenate(hot[2:], axis=0)], axis=1)
    place = me_x ^ jnp.arange(gx, dtype=i32)
    hot = hot[place // 2 + (gx // 2) * (place % 2)]
    hot = jnp.swapaxes(hot, 1, 2).reshape(hot_rows, feats)[:, :width]
    return in_t[:width].T, out_t[:width].T, hot


def solution(mesh):
    placed = (
        P(axes, None),
        P(axes, None),
        P(),
        P(None, axes, None),
        P(None, axes),
        P(None, axes, None),
        P(None, axes, None),
        P(None, axes),
        P(None, axes, None),
        P(None, axes),
        P(None, axes),
    )
    return jax.shard_map(
        body,
        mesh=mesh,
        in_specs=placed,
        out_specs=(P(axes, None), P(axes, None), P()),
        check_vma=False,
    )
```

```python
import functools
import jax
import jax.numpy as jnp
from jax import lax
from jax.experimental import pallas as pl
from jax.experimental.pallas import tpu as pltpu
from jax.sharding import PartitionSpec as P

learn_rate = 2.0
exact = lax.Precision.HIGHEST
axes = ("gx", "gy")
LANES = 128
SLOTS = 8
META = SLOTS + 16
GROUP = 4
f32, bf16, i32 = jnp.float32, jnp.bfloat16, jnp.int32
NN = (((1,), (0,)), ((), ()))
NT = (((1,), (1,)), ((), ()))
TN = (((0,), (0,)), ((), ()))


def swap(x, bit, devices):
    return lax.ppermute(x, axes, [(d, d ^ bit) for d in range(devices)])


def split3(x):
    hi = x.astype(bf16)
    rest = x - hi.astype(f32)
    mid = rest.astype(bf16)
    return hi, mid, (rest - mid.astype(f32)).astype(bf16)


def split2(x):
    hi = x.astype(bf16)
    return hi, (x - hi.astype(f32)).astype(bf16)


class Tree:
    def __init__(self, gx, gy):
        self.gx, self.gy = gx, gy
        self.devices = gx * gy
        self.low = [1 << b for b in range(gy.bit_length() - 1)]
        self.high = [gy << b for b in range(1, gx.bit_length() - 1)]
        self.core = gy

    def widen(self, parts, plans):
        m = len(plans[0])
        tails = [p.shape for p in parts]
        parts = [p.reshape((1,) * m + p.shape) for p in parts]
        for k in range(m):
            got = yield parts, [swap(p, plan[k][0], self.devices) for p, plan in zip(parts, plans)]
            parts = [jnp.concatenate([p, g], axis=plan[k][1]) for p, g, plan in zip(parts, got, plans)]
        return [p.reshape((-1,) + t) for p, t in zip(parts, tails)]

    def plans(self):
        mh, ml = len(self.high), len(self.low)
        low = [(self.low[b], ml - 1 - b) for b in reversed(range(ml))]
        high = [(self.high[b], mh - 1 - b) for b in range(mh)]
        return low, [high, high[::-1]]

    def gather(self, x):
        low, _ = self.plans()
        (x,) = yield from self.widen([x], [low])
        h = x.shape[1] // 2
        return (yield from self.gather_gx(x[:, :h], x[:, h:]))

    def gather_gx(self, a, b):
        _, high = self.plans()
        x, y = yield from self.widen([a, b], high)
        x, y = [v.reshape((-1,) + v.shape[2:]) for v in (x, y)]
        got = yield [x, y], [swap(x, self.core, self.devices), swap(y, self.core, self.devices)]
        return [x, got[0], y, got[1]]

    def gather_one(self, x):
        low, high = self.plans()
        (x,) = yield from self.widen([x], [low])
        (x,) = yield from self.widen([x], high[:1])
        x = x.reshape((-1,) + x.shape[2:])
        got = yield [x], [swap(x, self.core, self.devices)]
        return jnp.concatenate([x, got[0]], axis=0)

    def reduce(self, a0, a1, b0, b1):
        got = yield [a1, b1], [swap(a1, self.core, self.devices), swap(b1, self.core, self.devices)]
        low, high = self.plans()
        shape = (2,) * len(high[0]) + (self.gy,) + a0.shape[1:]
        parts = [(a0 + got[0]).reshape(shape), (b0 + got[1]).reshape(shape)]
        parts = yield from self.fold(parts, [plan[::-1] for plan in high])
        x = jnp.concatenate([p.reshape(p.shape[-3:]) for p in parts], axis=1)
        (x,) = yield from self.fold([x.reshape((2,) * len(low) + x.shape[1:])], [low[::-1]])
        return x.reshape(x.shape[-2:])

    def fold(self, parts, plans):
        for k in range(len(plans[0])):
            near = [lax.slice_in_dim(p, 0, 1, axis=plan[k][1]) for p, plan in zip(parts, plans)]
            far = [lax.slice_in_dim(p, 1, 2, axis=plan[k][1]) for p, plan in zip(parts, plans)]
            got = yield far, [swap(p, plan[k][0], self.devices) for p, plan in zip(far, plans)]
            parts = [p + g for p, g in zip(near, got)]
        return parts

    def place_of(self, mask):
        bits = self.devices.bit_length() - 1
        g, low = mask // self.gy, mask % self.gy
        return (g % 2) * (1 << (bits - 1)) + (g // 2) * self.gy + low

    def slice_mask(self, place):
        half = self.gx // 2
        return place // half + 2 * (place % half)


def params(*semantics):
    return pltpu.CompilerParams(dimension_semantics=semantics, vmem_limit_bytes=40 * 2**20)


def cost(flops, nbytes, trans=0):
    return pl.CostEstimate(flops=int(flops), bytes_accessed=int(nbytes), transcendentals=int(trans))


def after(x, *earlier):
    return lax.optimization_barrier((x, earlier))[0]


class Lane:
    def __init__(self, chain, stages):
        self.chain, self.left = chain, stages
        self.sent, self.got = next(chain)


def stage(lanes, fill=None):
    lanes = [lane for lane in lanes if lane is not None and lane.left > 0]
    sent = [lane.sent for lane in lanes]
    beside = fill(lambda x: after(x, sent)) if fill is not None else ()
    got, beside = lax.optimization_barrier(([lane.got for lane in lanes], beside))
    for lane, arrived in zip(lanes, got):
        lane.left -= 1
        try:
            lane.sent, lane.got = lane.chain.send(arrived)
        except StopIteration as end:
            lane.result = end.value
    return beside


def count_kernel(ids_ref, out_ref):
    groups = out_ref.shape[1]
    for s in range(out_ref.shape[0]):
        ids = ids_ref[s:s + 1, :]
        n = ids.shape[1]
        high = jnp.where(lax.broadcasted_iota(i32, (groups, n), 0) == ids // LANES, 1.0, 0.0)
        low = jnp.where(lax.broadcasted_iota(i32, (LANES, n), 0) == ids % LANES, 1.0, 0.0)
        total = lax.dot_general(high.astype(bf16), low.astype(bf16), NT, preferred_element_type=f32)
        out_ref[s] = total.astype(i32)


def count(ids, hot_rows):
    return pl.pallas_call(
        count_kernel,
        out_shape=jax.ShapeDtypeStruct((ids.shape[0], hot_rows // LANES, LANES), i32),
        compiler_params=pltpu.CompilerParams(vmem_limit_bytes=40 * 2**20),
        cost_estimate=cost(1e6, 1e5),
        name="count",
    )(ids)


def count_row(rows_ref, slice_at, width):
    at = SLOTS + slice_at * (width // LANES)
    rows = [rows_ref[pl.ds(at + q, 1), :] for q in range(width // LANES)]
    return jnp.concatenate(rows, axis=1).astype(f32)


def couple_kernel(own_ref, other_ref, in_ref, out_ref, wide):
    @pl.when(pl.program_id(0) == 0)
    def _():
        for k in range(SLOTS):
            wide[k] = jnp.broadcast_to(own_ref[0, :, k:k + 1], wide.shape[1:])

    for c in range(2):
        total = jnp.zeros(wide.shape[1:], f32)
        for k in range(SLOTS - 1):
            row = other_ref[c, 0, 0, k:k + 1, :]
            in_bag = wide[1] == row
            for j in range(2, SLOTS - 1):
                in_bag = in_bag | (wide[j] == row)
            total = total + jnp.where(in_bag, 1.0, 0.0) + jnp.where(wide[0] == row, 1.0, 0.0)
        in_ref[c, 0] = total.astype(bf16)
        same = wide[SLOTS - 1] == other_ref[c, 0, 0, SLOTS - 1:SLOTS, :]
        out_ref[c, 0] = jnp.where(same, 1.0, 0.0).astype(bf16)


def couple(own, meta, later, earlier):
    half, n = meta.shape[1], own.shape[1]
    shape = jax.ShapeDtypeStruct((2, half, n, n), bf16)
    spec = pl.BlockSpec((2, 1, n, n), lambda p: (0, p, 0, 0))
    return pl.pallas_call(
        couple_kernel,
        out_shape=(shape, shape),
        grid=(half,),
        in_specs=[
            pl.BlockSpec((1, n, SLOTS), lambda p: (later, 0, 0)),
            pl.BlockSpec((2, 1, 1, META, LANES), lambda p: (0, p, earlier, 0, 0)),
        ],
        out_specs=(spec, spec),
        scratch_shapes=[pltpu.VMEM((SLOTS, n, n), i32)],
        compiler_params=params("arbitrary"),
        cost_estimate=cost(half * 2 * n * n * 150, half * n * n * 8),
        name="couple",
    )(own, meta)


def local_rows(ids, rows, context):
    if context:
        return [ids[SLOTS - 1:SLOTS, :]]
    ids = jnp.where((ids >= 0) & (ids < rows), ids, -1)
    return [ids[0:1, :], jnp.max(ids[1:SLOTS - 1, :], axis=0, keepdims=True)]


def base_kernel(rows, base_ref, meta_ref, table_ref, a0, a1, b0, b1, parts):
    feats = table_ref.shape[0]

    @pl.when(pl.program_id(0) == 0)
    def _():
        for k, part in enumerate(split3(table_ref[...])):
            parts[k * feats:(k + 1) * feats, :] = part

    h = a0.shape[1]
    iota = lax.broadcasted_iota(i32, (rows, LANES), 0)
    for p in range(a0.shape[0]):
        picks = []
        for c in range(2):
            one, two = local_rows(meta_ref[c, p, 0, :SLOTS, :] - base_ref[0], rows, False)
            picks.append(jnp.where(iota == one, 1.0, 0.0) + jnp.where(iota == two, 1.0, 0.0))
        pick = jnp.concatenate(picks, axis=1).astype(bf16)
        total = jnp.dot(parts[...], pick, preferred_element_type=f32)
        total = total[:feats] + total[feats:2 * feats] + total[2 * feats:]
        a0[p] = total[:h, :LANES]
        a1[p] = total[:h, LANES:]
        b0[p] = total[h:, :LANES]
        b1[p] = total[h:, LANES:]


def base_sums(table_t, meta, base, step):
    half = meta.shape[1]
    feats, rows = table_t.shape
    shape = jax.ShapeDtypeStruct((half, feats // 2, LANES), f32)
    spec = pl.BlockSpec((GROUP, feats // 2, LANES), lambda p, b: (p, 0, 0))
    return pl.pallas_call(
        functools.partial(base_kernel, rows),
        out_shape=(shape,) * 4,
        grid_spec=pltpu.PrefetchScalarGridSpec(
            num_scalar_prefetch=1,
            grid=(half // GROUP,),
            in_specs=[
                pl.BlockSpec((2, GROUP, 1, META, LANES), lambda p, b: (0, p, step, 0, 0)),
                pl.BlockSpec((feats, rows), lambda p, b: (0, 0)),
            ],
            out_specs=(spec,) * 4,
            scratch_shapes=[pltpu.VMEM((3 * feats, rows), bf16)],
        ),
        compiler_params=params("arbitrary"),
        cost_estimate=cost(2 * 3 * half * 256 * feats * rows, half * 2 * feats * 512 + feats * rows * 4),
        name="base_sums",
    )(base, meta, table_t)


def tokens_of(r0, r1):
    return jnp.concatenate([r[p] for p in range(r0.shape[0]) for r in (r0, r1)], axis=1)


def update_kernel(rows, width, context, final, base_ref, meta_ref, table_ref, *refs):
    if final:
        result, pick, out_ref = refs[-3:]
    else:
        out_ref, pick = refs[-2:]
    ga0, ga1, gb0, gb1 = refs[:4]

    @pl.when(pl.program_id(0) == 0)
    def _():
        out_ref[...] = table_ref[...]

    iota = lax.broadcasted_iota(i32, (LANES, rows), 1)
    for p in range(ga0.shape[0]):
        for c in range(2):
            ids = meta_ref[c, p, 0, :SLOTS, :] - base_ref[0]
            found = local_rows(ids, rows, context)
            found = jnp.concatenate(found + [found[0]] * (SLOTS - len(found)), axis=0).T
            hits = jnp.where(iota == found[:, 0:1], 1.0, 0.0)
            if not context:
                hits = hits + jnp.where(iota == found[:, 1:2], 1.0, 0.0)
            at = (2 * p + c) * LANES
            pick[at:at + LANES, :] = hits.astype(bf16)
    ga, gb = tokens_of(ga0, ga1), tokens_of(gb0, gb1)
    if context:
        pos0, pos1 = refs[4], refs[5]
        row = width - gb.shape[0]
        pos = jnp.concatenate(
            [r[p, row:row + 1, :] for p in range(pos0.shape[0]) for r in (pos0, pos1)], axis=1
        )
        ga, gb = ga * pos, gb * pos
    grad = jnp.concatenate([ga, gb], axis=0) * learn_rate
    feats = grad.shape[0]
    both = jnp.concatenate(split2(grad), axis=0)
    total = jnp.dot(both, pick[...], preferred_element_type=f32)
    out_ref[...] = out_ref[...] - (total[:feats] + total[feats:])
    if final:

        @pl.when(pl.program_id(0) == pl.num_programs(0) - 1)
        def _():
            result[...] = out_ref[...].T[:, :width]


def update(table_t, meta, base, step, width, g, pos=(), final=False):
    half = meta.shape[1]
    feats, rows = table_t.shape
    piece = pl.BlockSpec((GROUP, feats // 2, LANES), lambda p, b: (p, 0, 0))
    whole = pl.BlockSpec((feats, rows), lambda p, b: (0, 0))
    arrays = list(g) + list(pos)
    return pl.pallas_call(
        functools.partial(update_kernel, rows, width, bool(pos), final),
        out_shape=jax.ShapeDtypeStruct((rows, width) if final else (feats, rows), f32),
        grid_spec=pltpu.PrefetchScalarGridSpec(
            num_scalar_prefetch=1,
            grid=(half // GROUP,),
            in_specs=[pl.BlockSpec((2, GROUP, 1, META, LANES), lambda p, b: (0, p, step, 0, 0)), whole]
            + [piece] * len(arrays),
            out_specs=pl.BlockSpec((rows, width), lambda p, b: (0, 0)) if final else whole,
            scratch_shapes=[pltpu.VMEM((GROUP * 2 * LANES, rows), bf16)]
            + ([pltpu.VMEM((feats, rows), f32)] if final else []),
        ),
        compiler_params=params("arbitrary"),
        cost_estimate=cost(2 * 2 * half * 256 * feats * rows, half * 2 * feats * 512 * len(arrays) // 4),
        name="context_update" if pos else "update",
    )(base, meta, table_t, *arrays)


def absorb_kernel(width, ga0, ga1, gb0, gb1, ca0, ca1, cb0, cb1, in_ref, ctx_ref, c_out, x_out):
    @pl.when(pl.program_id(0) == 0)
    def _():
        c_out[...] = jnp.zeros_like(c_out)
        x_out[...] = jnp.zeros_like(x_out)

    group = ga0.shape[0]
    ga, gb = tokens_of(ga0, ga1), tokens_of(gb0, gb1)
    row = width - gb.shape[0]
    pos = gb[row:row + 1, :]
    grad = jnp.concatenate([ga, gb], axis=0)
    centre = jnp.concatenate([tokens_of(ca0, ca1), tokens_of(cb0, cb1)], axis=0) * pos
    feats = grad.shape[0]
    for value, ref, out in ((grad, in_ref, c_out), (centre, ctx_ref, x_out)):
        pairs = jnp.concatenate([ref[c, p] for p in range(group) for c in range(2)], axis=1)
        parts = jnp.concatenate(split3(value * learn_rate), axis=0)
        total = lax.dot_general(parts, pairs, NT, preferred_element_type=f32)
        out[...] += total[:feats] + total[feats:2 * feats] + total[2 * feats:]


def absorb(width, g, c, in_pairs, ctx_pairs):
    half, feats_half, n = g[0].shape
    piece = pl.BlockSpec((GROUP, feats_half, n), lambda p: (p, 0, 0))
    pair = pl.BlockSpec((2, GROUP, n, n), lambda p: (0, p, 0, 0))
    shape = jax.ShapeDtypeStruct((2 * feats_half, n), f32)
    spec = pl.BlockSpec((2 * feats_half, n), lambda p: (0, 0))
    return pl.pallas_call(
        functools.partial(absorb_kernel, width),
        out_shape=(shape, shape),
        grid=(half // GROUP,),
        in_specs=[piece] * 8 + [pair] * 2,
        out_specs=(spec, spec),
        compiler_params=params("arbitrary"),
        cost_estimate=cost(2 * 2 * 3 * half * 256 * feats_half * 2 * n, half * 256 * feats_half * 16),
        name="absorb",
    )(*g, *c, in_pairs, ctx_pairs)


def dot6(left, right, dims):
    m = left[0].shape[0]
    one = lax.dot_general(jnp.concatenate(left, axis=0), right[0], dims, preferred_element_type=f32)
    two = lax.dot_general(jnp.concatenate(left[:2], axis=0), right[1], dims, preferred_element_type=f32)
    three = lax.dot_general(left[0], right[2], dims, preferred_element_type=f32)
    return one[:m] + (one[m:2 * m] + two[:m]) + ((one[2 * m:] + two[m:]) + three)


def own_kernel(width, scale, slice_ref, c_ref, x_ref, denom_ref, meta_ref, a0, a1, b0, b1, out_ref, total):
    p = pl.program_id(0)

    @pl.when(p == 0)
    def _():
        total[...] = jnp.zeros_like(total)

    centre = c_ref[...]
    group, hot_slice = a0.shape[0], a0.shape[2]
    hot = jnp.concatenate([tokens_of(a0, a1), tokens_of(b0, b1)], axis=0)
    half = pl.num_programs(0) * group
    counts = [
        count_row(meta_ref.at[0], slice_ref[c * half + p * group + q], hot_slice)
        for q in range(group)
        for c in range(2)
    ]
    counts = jnp.concatenate(counts, axis=1)
    parts = split3(hot)
    scores = dot6(split3(centre.T), parts, NN)
    grad = (scale * counts) * jax.nn.sigmoid(scores)
    total[...] += dot6(parts, split3(grad), NT)

    @pl.when(p == pl.num_programs(0) - 1)
    def _():
        context = x_ref[...]
        positive = jnp.sum(centre * context, axis=0, keepdims=True)
        pos = jax.nn.sigmoid(positive) - 1.0
        grad = (pos * context + total[...]) / denom_ref[...]
        feature = lax.broadcasted_iota(i32, grad.shape, 0)
        out_ref[...] = jnp.where(feature == width, pos, grad)


def own_grads(width, scale, centre, context, denom, slice_of, meta, step, hot):
    feats, n = centre.shape
    half, feats_half, hot_slice = hot[0].shape
    group = max(1, 512 // hot_slice)
    whole = pl.BlockSpec((feats, n), lambda p, o: (0, 0))
    piece = pl.BlockSpec((group, feats_half, hot_slice), lambda p, o: (p, 0, 0))
    return pl.pallas_call(
        functools.partial(own_kernel, width, scale),
        out_shape=jax.ShapeDtypeStruct((feats, n), f32),
        grid_spec=pltpu.PrefetchScalarGridSpec(
            num_scalar_prefetch=1,
            grid=(half // group,),
            in_specs=[
                whole,
                whole,
                pl.BlockSpec((1, n), lambda p, o: (0, 0)),
                pl.BlockSpec((1, META, LANES), lambda p, o: (step, 0, 0)),
            ]
            + [piece] * 4,
            out_specs=whole,
            scratch_shapes=[pltpu.VMEM((feats, n), f32)],
        ),
        compiler_params=params("arbitrary"),
        cost_estimate=cost(2 * 2 * 6 * half * 2 * hot_slice * feats * n, half * 4 * feats_half * hot_slice * 4),
        name="own_grads",
    )(slice_of, centre, context, denom, meta, *hot)


def hot_kernel(scale, slice_ref, meta_ref, hot_a, hot_b, a, b, *refs):
    p = pl.program_id(0)
    total, parts = refs[-2:]
    first = len(refs) == 3

    @pl.when(p == 0)
    def _():
        total[...] = jnp.zeros_like(total) if first else refs[0][...]
        hot = jnp.concatenate([hot_a[0], hot_b[0]], axis=0)
        for k, part in enumerate(split3(hot)):
            parts[k] = part

    group, n = a.shape[0], a.shape[2]
    hot_slice = hot_a.shape[2]
    centre = jnp.concatenate(
        [jnp.concatenate([r[q] for q in range(group)], axis=1) for r in (a, b)], axis=0
    )
    scores = dot6(split3(centre.T), [parts[0], parts[1], parts[2]], NN)
    sums = []
    for q in range(0, group, 2):
        grads = []
        for r in (q, q + 1):
            counts = count_row(meta_ref.at[0, r, 0], slice_ref[0], hot_slice)
            grads.append((scale * counts) * jax.nn.sigmoid(scores[r * n:(r + 1) * n]))
        sums.append(dot6(split3(centre[:, q * n:(q + 2) * n]), split3(jnp.concatenate(grads, axis=0)), NN))
    while len(sums) > 1:
        sums = [x + y for x, y in zip(sums[::2], sums[1::2])]
    total[...] += sums[0]

    @pl.when(p == pl.num_programs(0) - 1)
    def _():
        if first:
            refs[0][...] = total[...]
        else:
            out_a, out_b = refs[1:3]
            h = out_a.shape[0]
            out_a[...] = hot_a[0] - learn_rate * total[:h, :]
            out_b[...] = hot_b[0] - learn_rate * total[h:, :]


def hot_update(scale, me_x, meta, step, hot, core, a, b, partial=None):
    half, feats_half, n = a.shape
    hot_slice = hot[0].shape[2]
    group = 2 * GROUP
    whole = pl.BlockSpec((2 * feats_half, hot_slice), lambda p, o: (0, 0))
    out = pl.BlockSpec((feats_half, hot_slice), lambda p, o: (0, 0))
    first = pl.BlockSpec((1, feats_half, hot_slice), lambda p, o: (0, 0, 0))
    piece = pl.BlockSpec((group, feats_half, n), lambda p, o: (p, 0, 0))
    sum_shape = jax.ShapeDtypeStruct((2 * feats_half, hot_slice), f32)
    half_shape = jax.ShapeDtypeStruct((feats_half, hot_slice), f32)
    return pl.pallas_call(
        functools.partial(hot_kernel, scale),
        out_shape=sum_shape if partial is None else (half_shape, half_shape),
        grid_spec=pltpu.PrefetchScalarGridSpec(
            num_scalar_prefetch=1,
            grid=(half // group,),
            in_specs=[
                pl.BlockSpec((1, group, 1, META, LANES), lambda p, o: (core, p, step, 0, 0)),
                first,
                first,
                piece,
                piece,
            ]
            + ([] if partial is None else [whole]),
            out_specs=whole if partial is None else (out, out),
            scratch_shapes=[
                pltpu.VMEM((2 * feats_half, hot_slice), f32),
                pltpu.VMEM((3, 2 * feats_half, hot_slice), bf16),
            ],
        ),
        compiler_params=params("arbitrary"),
        cost_estimate=cost(2 * 2 * 6 * half * 128 * hot_slice * feats_half * 2, half * 128 * feats_half * 8),
        name="hot_update",
    )(me_x, meta, hot[0], hot[2], a, b, *([] if partial is None else [partial]))


def spread_kernel(slice_ref, row0, row1, a0, a1, b0, b1):
    h = a0.shape[1]
    for row, a, b in ((row0, a0, b0), (row1, a1, b1)):
        turned = row[...].T
        a[0] = turned[:h]
        b[...] = jnp.zeros_like(b)
        b[0, :turned.shape[0] - h, :] = turned[h:]


def spread(hot_table, slice_of, feats):
    hot_rows, width = hot_table.shape
    count_of = slice_of.shape[0]
    half, hot_slice = count_of // 2, hot_rows // count_of
    shape = jax.ShapeDtypeStruct((half, feats // 2, hot_slice), f32)
    piece = pl.BlockSpec((1, feats // 2, hot_slice), lambda p, o: (p, 0, 0))
    return list(
        pl.pallas_call(
            spread_kernel,
            out_shape=(shape,) * 4,
            grid_spec=pltpu.PrefetchScalarGridSpec(
                num_scalar_prefetch=1,
                grid=(half,),
                in_specs=[
                    pl.BlockSpec((hot_slice, width), lambda p, o: (o[p], 0)),
                    pl.BlockSpec((hot_slice, width), lambda p, o: (o[half + p], 0)),
                ],
                out_specs=(piece,) * 4,
            ),
            compiler_params=params("arbitrary"),
            cost_estimate=cost(1e6, 2 * hot_rows * feats * 4),
            name="spread",
        )(slice_of, hot_table, hot_table)
    )


def collect_kernel(width, slice_ref, a0, a1, b0, b1, out):
    for c, (a, b) in enumerate(((a0, b0), (a1, b1))):

        @pl.when(pl.program_id(0) == c)
        def _():
            out[...] = jnp.concatenate([a[0], b[0]], axis=0).T[:, :width]


def collect(pieces, slice_of, width):
    half, feats_half, hot_slice = pieces[0].shape
    piece = pl.BlockSpec((1, feats_half, hot_slice), lambda c, p, o: (p, 0, 0))
    return pl.pallas_call(
        functools.partial(collect_kernel, width),
        out_shape=jax.ShapeDtypeStruct((2 * half * hot_slice, width), f32),
        grid_spec=pltpu.PrefetchScalarGridSpec(
            num_scalar_prefetch=1,
            grid=(2, half),
            in_specs=[piece] * 4,
            out_specs=pl.BlockSpec((hot_slice, width), lambda c, p, o: (o[c * half + p], 0)),
        ),
        compiler_params=params("arbitrary", "arbitrary"),
        cost_estimate=cost(1e6, 4 * half * feats_half * hot_slice * 8),
        name="collect",
    )(slice_of, *pieces)


def rows_to_send(tree, me, out_table, ids, cap):
    rows = out_table.shape[0]
    devices, steps, n = ids.shape
    ids = ids - me * rows
    mine = (ids >= 0) & (ids < rows)
    before = jnp.triu(jnp.ones((n, n), bf16), 1)
    rank = jnp.dot(mine.astype(bf16), before, preferred_element_type=f32).astype(i32)
    slots = jnp.arange(cap, dtype=i32)
    hit = mine[:, :, None, :] & (rank[:, :, None, :] == slots[None, None, :, None])
    wanted = jnp.sum(jnp.where(hit, ids[:, :, None, :], 0), axis=3)
    order = tree.place_of(me ^ jnp.arange(devices, dtype=i32))
    return out_table[wanted[order].reshape(devices, steps * cap)]


def rows_that_came(got, owner, cap):
    steps, n = owner.shape
    same = (owner[:, :, None] == owner[:, None, :]) & (
        jnp.arange(n)[None, :, None] > jnp.arange(n)[None, None, :]
    )
    own_rank = jnp.sum(same.astype(i32), axis=2)
    at = (owner * steps + jnp.arange(steps, dtype=i32)[:, None]) * cap + own_rank
    return got.reshape(-1, got.shape[2])[at]


def body(
    in_table,
    out_table,
    hot_table,
    centre_owner,
    centre_row,
    bag_owner,
    bag_row,
    bag_len,
    context_owner,
    context_row,
    negative_ids,
):
    gx, gy = lax.axis_size("gx"), lax.axis_size("gy")
    tree = Tree(gx, gy)
    devices = tree.devices
    me_x = lax.axis_index("gx").astype(i32)
    me = me_x * gy + lax.axis_index("gy").astype(i32)
    steps, n, bag = bag_row.shape
    rows, width = in_table.shape
    out_rows = out_table.shape[0]
    hot_rows = hot_table.shape[0]
    neg = negative_ids.shape[1]
    cap = max(2, 2 * n // devices)
    hot_slice = hot_rows // gx
    feats = -(-(width + 1) // 16) * 16
    h = feats // 2
    scale = 16.0 / neg

    kept = jnp.arange(bag, dtype=i32)[None, None, :] < bag_len[:, :, None]
    centre_ids = centre_owner * rows + centre_row[:, :, None]
    bag_ids = bag_owner * rows + bag_row
    context_ids = context_owner * out_rows + context_row[:, :, None]
    own = jnp.concatenate([centre_ids, jnp.where(kept, bag_ids, -2), context_ids], axis=2)
    sent = jnp.concatenate([centre_ids, jnp.where(kept, bag_ids, -1), context_ids], axis=2)
    meta = jnp.concatenate([jnp.swapaxes(sent, 1, 2), count(negative_ids, hot_rows)], axis=1)
    span = len(tree.low) + len(tree.high) + 1
    short = len(tree.high) + 1
    lane = Lane(tree.gather_one(meta.reshape(steps * META, LANES)), span)
    while lane.left:
        stage([lane])
    meta_flat = lane.result.reshape(devices, steps, META, LANES)
    meta_all = meta_flat.reshape(2, devices // 2, steps, META, LANES)

    small = devices > 64
    in_base = (me * rows).reshape(1)
    out_base = (me * out_rows).reshape(1)
    spare = ((0, feats - width), (0, 0))
    in_t = jnp.pad(in_table.T, spare)
    source = in_t
    part = base_sums(source, meta_all, in_base, 0)
    hot_late, out_late = after((hot_table, out_table), part[0])
    out_t = jnp.pad(out_late.T, spare)
    slice_of = me_x ^ tree.slice_mask(jnp.arange(gx, dtype=i32))
    hot = spread(hot_late, slice_of, feats)
    denom = 1.0 + bag_len.astype(f32)

    def sums(s):
        return lambda gate: base_sums(gate(source), meta_all, in_base, s)

    def pair(later, e):
        return lambda gate: couple(gate(own), meta_all, later, e)

    def run(lanes, fills, kept, until):
        while until.left:
            name, fill = fills.pop(0) if fills else (None, None)
            beside = stage(lanes, fill)
            if name is not None:
                kept[name] = beside

    def requests(gate):
        return rows_to_send(tree, me, gate(out_table), meta_flat[:, :, SLOTS - 1, :], cap)

    kept = {}
    lane = Lane(tree.reduce(*part), span)
    fills = [(("rows",), requests)]
    if not small and steps > 1:
        fills.insert(0, (("sums", 1), sums(1)))
    run([lane], fills, kept, lane)
    base = [lane.result] + [None] * (steps - 1)
    got = lax.all_to_all(kept.pop(("rows",)), axes, split_axis=0, concat_axis=0, tiled=True)
    got = rows_that_came(got, context_owner[:, :, 0], cap)
    context = [jnp.pad(got[k].T, spare) for k in range(steps)]
    real = jnp.arange(feats)[:, None] < width
    held = []
    added = [[] for _ in range(steps)]
    tables = [in_t, out_t]

    def grow(s, which):
        def fill(gate):
            g, c = held[s]
            final = s + 1 == steps
            if which == 0:
                return update(gate(tables[0]), meta_all, in_base, s, width, g, (), final)
            return update(gate(tables[1]), meta_all, out_base, s, width, c, g[2:], final)

        return fill

    def soak(later, e):
        def fill(gate):
            g, c = held[e]
            return absorb(width, [gate(g[0])] + g[1:], c, *kept[("pair", later, e)])

        return fill

    for s in range(steps):
        last = s + 1 == steps
        centre = jnp.where(real, base[s] / denom[s][None, :], 0.0)
        c_lane = Lane(tree.gather(centre), span)
        g = stage(
            [c_lane],
            lambda gate: own_grads(
                width, scale, gate(centre), context[s], denom[s][None, :], slice_of, meta, s, hot
            ),
        )
        g_lane = Lane(tree.gather(g), span)
        fills = []
        if not small:
            if s > 0:
                fills.append((("table", 1), grow(s - 1, 1)))
            if not last:
                fills.append((("pair", s + 1, s), pair(s + 1, s)))
            for later in range(s + 2, steps):
                fills.append((("sums", later), sums(later)) if later == s + 2 else (None, None))
            if s > 0:
                fills.append((("table", 0), grow(s - 1, 0)))
        if len(fills) == 2:
            fills.insert(1, (None, None))
        r_lane = None
        while c_lane.left:
            if c_lane.left == 1:
                kept.update((name, fill(lambda x: x)) for name, fill in fills if name is not None)
                for e in range(s):
                    if not small and not last:
                        kept[("pair", s + 1, e)] = couple(after(own, c_lane.sent[0]), meta_all, s + 1, e)
                if not small and not last:
                    r_lane = Lane(tree.reduce(*kept.pop(("sums", s + 1))), span)
                half_sum = stage(
                    [c_lane, g_lane, r_lane],
                    lambda gate: hot_update(
                        scale, me_x.reshape(1), meta_all, s, hot, 0, gate(c_lane.sent[0]), c_lane.sent[1]
                    ),
                )
                continue
            name, fill = fills.pop(0) if fills else (None, None)
            beside = stage([c_lane, g_lane, r_lane], fill)
            if name is not None:
                kept[name] = beside
        for which in (0, 1):
            tables[which] = kept.pop(("table", which), tables[which])
        c = c_lane.result
        new_a, new_b = stage(
            [g_lane, r_lane],
            lambda gate: hot_update(scale, me_x.reshape(1), meta_all, s, hot, 1, gate(c[1]), c[3], half_sum),
        )
        while g_lane.left:
            stage([g_lane, r_lane])
        held.append((g_lane.result, c))
        h_lane = Lane(tree.gather_gx(new_a[None], new_b[None]), short)
        due = [(later, s) for later in range(s + 1, steps)] if small else [(s + 1, e) for e in range(s, -1, -1)]
        due = [] if last else due
        if small:
            for later, e in due:
                kept[("pair", later, e)] = couple(own, meta_all, later, e)
        fills = [(("soak", later, e), soak(later, e)) for later, e in due]
        if last or small:
            fills += [(("table", 1), grow(s, 1)), (("table", 0), grow(s, 0))]
        run([h_lane, r_lane], fills, kept, h_lane)
        for name, fill in fills:
            kept[name] = fill(lambda x: x)
        for which in (0, 1):
            tables[which] = kept.pop(("table", which), tables[which])
        for later, e in due:
            added[later].append(kept.pop(("soak", later, e)))
        hot = h_lane.result
        if not last:
            if small:
                source, tables, hot, context, added = lax.optimization_barrier(
                    (source, tables, hot, context, added)
                )
                r_lane = Lane(tree.reduce(*base_sums(source, meta_all, in_base, s + 1)), span)
            while r_lane.left:
                stage([r_lane])
            base[s + 1] = r_lane.result
            for centre_add, context_add in added[s + 1]:
                base[s + 1] = base[s + 1] - centre_add
                context[s + 1] = context[s + 1] - context_add
    return tables[0], tables[1], collect(hot, slice_of, width)


def solution(mesh):
    placed = (
        P(axes, None),
        P(axes, None),
        P(),
        P(None, axes, None),
        P(None, axes),
        P(None, axes, None),
        P(None, axes, None),
        P(None, axes),
        P(None, axes, None),
        P(None, axes),
        P(None, axes),
    )
    return jax.shard_map(
        body,
        mesh=mesh,
        in_specs=placed,
        out_specs=(P(axes, None), P(axes, None), P()),
        check_vma=False,
    )
```

```python
import functools
import jax
import jax.numpy as jnp
from jax import lax
from jax.experimental import pallas as pl
from jax.experimental.pallas import tpu as pltpu
from jax.sharding import PartitionSpec as P

learn_rate = 2.0
exact = lax.Precision.HIGHEST
axes = ("gx", "gy")
LANES = 128
SLOTS = 8
META = SLOTS + 16
GROUP = 4
f32, bf16, i32 = jnp.float32, jnp.bfloat16, jnp.int32
NN = (((1,), (0,)), ((), ()))
NT = (((1,), (1,)), ((), ()))
TN = (((0,), (0,)), ((), ()))


def swap(x, bit, devices):
    return lax.ppermute(x, axes, [(d, d ^ bit) for d in range(devices)])


def split3(x):
    hi = x.astype(bf16)
    rest = x - hi.astype(f32)
    mid = rest.astype(bf16)
    return hi, mid, (rest - mid.astype(f32)).astype(bf16)


def split2(x):
    hi = x.astype(bf16)
    return hi, (x - hi.astype(f32)).astype(bf16)


class Tree:
    def __init__(self, gx, gy):
        self.gx, self.gy = gx, gy
        self.devices = gx * gy
        self.low = [1 << b for b in range(gy.bit_length() - 1)]
        self.high = [gy << b for b in range(1, gx.bit_length() - 1)]
        self.core = gy

    def widen(self, parts, plans):
        m = len(plans[0])
        tails = [p.shape for p in parts]
        parts = [p.reshape((1,) * m + p.shape) for p in parts]
        for k in range(m):
            got = yield parts, [swap(p, plan[k][0], self.devices) for p, plan in zip(parts, plans)]
            parts = [jnp.concatenate([p, g], axis=plan[k][1]) for p, g, plan in zip(parts, got, plans)]
        return [p.reshape((-1,) + t) for p, t in zip(parts, tails)]

    def plans(self):
        mh, ml = len(self.high), len(self.low)
        low = [(self.low[b], ml - 1 - b) for b in reversed(range(ml))]
        high = [(self.high[b], mh - 1 - b) for b in range(mh)]
        return low, [high, high[::-1]]

    def gather(self, x):
        low, _ = self.plans()
        (x,) = yield from self.widen([x], [low])
        h = x.shape[1] // 2
        return (yield from self.gather_gx(x[:, :h], x[:, h:]))

    def gather_gx(self, a, b):
        _, high = self.plans()
        x, y = yield from self.widen([a, b], high)
        x, y = [v.reshape((-1,) + v.shape[2:]) for v in (x, y)]
        got = yield [x, y], [swap(x, self.core, self.devices), swap(y, self.core, self.devices)]
        return [x, got[0], y, got[1]]

    def gather_one(self, x):
        low, high = self.plans()
        (x,) = yield from self.widen([x], [low])
        (x,) = yield from self.widen([x], high[:1])
        x = x.reshape((-1,) + x.shape[2:])
        got = yield [x], [swap(x, self.core, self.devices)]
        return jnp.concatenate([x, got[0]], axis=0)

    def reduce(self, a0, a1, b0, b1):
        got = yield [a1, b1], [swap(a1, self.core, self.devices), swap(b1, self.core, self.devices)]
        low, high = self.plans()
        shape = (2,) * len(high[0]) + (self.gy,) + a0.shape[1:]
        parts = [(a0 + got[0]).reshape(shape), (b0 + got[1]).reshape(shape)]
        parts = yield from self.fold(parts, [plan[::-1] for plan in high])
        x = jnp.concatenate([p.reshape(p.shape[-3:]) for p in parts], axis=1)
        (x,) = yield from self.fold([x.reshape((2,) * len(low) + x.shape[1:])], [low[::-1]])
        return x.reshape(x.shape[-2:])

    def fold(self, parts, plans):
        for k in range(len(plans[0])):
            near = [lax.slice_in_dim(p, 0, 1, axis=plan[k][1]) for p, plan in zip(parts, plans)]
            far = [lax.slice_in_dim(p, 1, 2, axis=plan[k][1]) for p, plan in zip(parts, plans)]
            got = yield far, [swap(p, plan[k][0], self.devices) for p, plan in zip(far, plans)]
            parts = [p + g for p, g in zip(near, got)]
        return parts

    def place_of(self, mask):
        bits = self.devices.bit_length() - 1
        g, low = mask // self.gy, mask % self.gy
        return (g % 2) * (1 << (bits - 1)) + (g // 2) * self.gy + low

    def slice_mask(self, place):
        half = self.gx // 2
        return place // half + 2 * (place % half)


def params(*semantics):
    return pltpu.CompilerParams(dimension_semantics=semantics, vmem_limit_bytes=40 * 2**20)


def cost(flops, nbytes, trans=0):
    return pl.CostEstimate(flops=int(flops), bytes_accessed=int(nbytes), transcendentals=int(trans))


def after(x, *earlier):
    return lax.optimization_barrier((x, earlier))[0]


class Lane:
    def __init__(self, chain, stages):
        self.chain, self.left = chain, stages
        self.sent, self.got = next(chain)


def stage(lanes, fill=None):
    lanes = [lane for lane in lanes if lane is not None and lane.left > 0]
    sent = [lane.sent for lane in lanes]
    beside = fill(lambda x: after(x, sent)) if fill is not None else ()
    got, beside = lax.optimization_barrier(([lane.got for lane in lanes], beside))
    for lane, arrived in zip(lanes, got):
        lane.left -= 1
        try:
            lane.sent, lane.got = lane.chain.send(arrived)
        except StopIteration as end:
            lane.result = end.value
    return beside


def count_kernel(ids_ref, out_ref):
    groups = out_ref.shape[1]
    for s in range(out_ref.shape[0]):
        ids = ids_ref[s:s + 1, :]
        n = ids.shape[1]
        high = jnp.where(lax.broadcasted_iota(i32, (groups, n), 0) == ids // LANES, 1.0, 0.0)
        low = jnp.where(lax.broadcasted_iota(i32, (LANES, n), 0) == ids % LANES, 1.0, 0.0)
        total = lax.dot_general(high.astype(bf16), low.astype(bf16), NT, preferred_element_type=f32)
        out_ref[s] = total.astype(i32)


def count(ids, hot_rows):
    return pl.pallas_call(
        count_kernel,
        out_shape=jax.ShapeDtypeStruct((ids.shape[0], hot_rows // LANES, LANES), i32),
        compiler_params=pltpu.CompilerParams(vmem_limit_bytes=40 * 2**20),
        cost_estimate=cost(1e6, 1e5),
        name="count",
    )(ids)


def count_row(rows_ref, slice_at, width):
    at = SLOTS + slice_at * (width // LANES)
    rows = [rows_ref[pl.ds(at + q, 1), :] for q in range(width // LANES)]
    return jnp.concatenate(rows, axis=1).astype(f32)


def couple_kernel(own_ref, other_ref, in_ref, out_ref, wide):
    @pl.when(pl.program_id(0) == 0)
    def _():
        for k in range(SLOTS):
            wide[k] = jnp.broadcast_to(own_ref[0, :, k:k + 1], wide.shape[1:])

    for c in range(2):
        total = jnp.zeros(wide.shape[1:], f32)
        for k in range(SLOTS - 1):
            row = other_ref[c, 0, 0, k:k + 1, :]
            in_bag = wide[1] == row
            for j in range(2, SLOTS - 1):
                in_bag = in_bag | (wide[j] == row)
            total = total + jnp.where(in_bag, 1.0, 0.0) + jnp.where(wide[0] == row, 1.0, 0.0)
        in_ref[c, 0] = total.astype(bf16)
        same = wide[SLOTS - 1] == other_ref[c, 0, 0, SLOTS - 1:SLOTS, :]
        out_ref[c, 0] = jnp.where(same, 1.0, 0.0).astype(bf16)


def couple(own, meta, later, earlier):
    half, n = meta.shape[1], own.shape[1]
    shape = jax.ShapeDtypeStruct((2, half, n, n), bf16)
    spec = pl.BlockSpec((2, 1, n, n), lambda p: (0, p, 0, 0))
    return pl.pallas_call(
        couple_kernel,
        out_shape=(shape, shape),
        grid=(half,),
        in_specs=[
            pl.BlockSpec((1, n, SLOTS), lambda p: (later, 0, 0)),
            pl.BlockSpec((2, 1, 1, META, LANES), lambda p: (0, p, earlier, 0, 0)),
        ],
        out_specs=(spec, spec),
        scratch_shapes=[pltpu.VMEM((SLOTS, n, n), i32)],
        compiler_params=params("arbitrary"),
        cost_estimate=cost(half * 2 * n * n * 150, half * n * n * 8),
        name="couple",
    )(own, meta)


def local_rows(ids, rows, context):
    if context:
        return [ids[SLOTS - 1:SLOTS, :]]
    ids = jnp.where((ids >= 0) & (ids < rows), ids, -1)
    return [ids[0:1, :], jnp.max(ids[1:SLOTS - 1, :], axis=0, keepdims=True)]


def base_kernel(rows, base_ref, meta_ref, table_ref, a0, a1, b0, b1, parts):
    feats = table_ref.shape[0]

    @pl.when(pl.program_id(0) == 0)
    def _():
        for k, part in enumerate(split3(table_ref[...])):
            parts[k * feats:(k + 1) * feats, :] = part

    h = a0.shape[1]
    iota = lax.broadcasted_iota(i32, (rows, LANES), 0)
    for p in range(a0.shape[0]):
        picks = []
        for c in range(2):
            one, two = local_rows(meta_ref[c, p, 0, :SLOTS, :] - base_ref[0], rows, False)
            picks.append(jnp.where(iota == one, 1.0, 0.0) + jnp.where(iota == two, 1.0, 0.0))
        pick = jnp.concatenate(picks, axis=1).astype(bf16)
        total = jnp.dot(parts[...], pick, preferred_element_type=f32)
        total = total[:feats] + total[feats:2 * feats] + total[2 * feats:]
        a0[p] = total[:h, :LANES]
        a1[p] = total[:h, LANES:]
        b0[p] = total[h:, :LANES]
        b1[p] = total[h:, LANES:]


def base_sums(table_t, meta, base, step):
    half = meta.shape[1]
    feats, rows = table_t.shape
    shape = jax.ShapeDtypeStruct((half, feats // 2, LANES), f32)
    spec = pl.BlockSpec((GROUP, feats // 2, LANES), lambda p, b: (p, 0, 0))
    return pl.pallas_call(
        functools.partial(base_kernel, rows),
        out_shape=(shape,) * 4,
        grid_spec=pltpu.PrefetchScalarGridSpec(
            num_scalar_prefetch=1,
            grid=(half // GROUP,),
            in_specs=[
                pl.BlockSpec((2, GROUP, 1, META, LANES), lambda p, b: (0, p, step, 0, 0)),
                pl.BlockSpec((feats, rows), lambda p, b: (0, 0)),
            ],
            out_specs=(spec,) * 4,
            scratch_shapes=[pltpu.VMEM((3 * feats, rows), bf16)],
        ),
        compiler_params=params("arbitrary"),
        cost_estimate=cost(2 * 3 * half * 256 * feats * rows, half * 2 * feats * 512 + feats * rows * 4),
        name="base_sums",
    )(base, meta, table_t)


def tokens_of(r0, r1):
    return jnp.concatenate([r[p] for p in range(r0.shape[0]) for r in (r0, r1)], axis=1)


def update_kernel(rows, width, context, final, base_ref, meta_ref, table_ref, *refs):
    if final:
        result, pick, out_ref = refs[-3:]
    else:
        out_ref, pick = refs[-2:]
    ga0, ga1, gb0, gb1 = refs[:4]

    @pl.when(pl.program_id(0) == 0)
    def _():
        out_ref[...] = table_ref[...]

    iota = lax.broadcasted_iota(i32, (LANES, rows), 1)
    for p in range(ga0.shape[0]):
        for c in range(2):
            ids = meta_ref[c, p, 0, :SLOTS, :] - base_ref[0]
            found = local_rows(ids, rows, context)
            found = jnp.concatenate(found + [found[0]] * (SLOTS - len(found)), axis=0).T
            hits = jnp.where(iota == found[:, 0:1], 1.0, 0.0)
            if not context:
                hits = hits + jnp.where(iota == found[:, 1:2], 1.0, 0.0)
            at = (2 * p + c) * LANES
            pick[at:at + LANES, :] = hits.astype(bf16)
    ga, gb = tokens_of(ga0, ga1), tokens_of(gb0, gb1)
    if context:
        pos0, pos1 = refs[4], refs[5]
        row = width - gb.shape[0]
        pos = jnp.concatenate(
            [r[p, row:row + 1, :] for p in range(pos0.shape[0]) for r in (pos0, pos1)], axis=1
        )
        ga, gb = ga * pos, gb * pos
    grad = jnp.concatenate([ga, gb], axis=0) * learn_rate
    feats = grad.shape[0]
    both = jnp.concatenate(split2(grad), axis=0)
    total = jnp.dot(both, pick[...], preferred_element_type=f32)
    out_ref[...] = out_ref[...] - (total[:feats] + total[feats:])
    if final:

        @pl.when(pl.program_id(0) == pl.num_programs(0) - 1)
        def _():
            result[...] = out_ref[...].T[:, :width]


def update(table_t, meta, base, step, width, g, pos=(), final=False):
    half = meta.shape[1]
    feats, rows = table_t.shape
    piece = pl.BlockSpec((GROUP, feats // 2, LANES), lambda p, b: (p, 0, 0))
    whole = pl.BlockSpec((feats, rows), lambda p, b: (0, 0))
    arrays = list(g) + list(pos)
    return pl.pallas_call(
        functools.partial(update_kernel, rows, width, bool(pos), final),
        out_shape=jax.ShapeDtypeStruct((rows, width) if final else (feats, rows), f32),
        grid_spec=pltpu.PrefetchScalarGridSpec(
            num_scalar_prefetch=1,
            grid=(half // GROUP,),
            in_specs=[pl.BlockSpec((2, GROUP, 1, META, LANES), lambda p, b: (0, p, step, 0, 0)), whole]
            + [piece] * len(arrays),
            out_specs=pl.BlockSpec((rows, width), lambda p, b: (0, 0)) if final else whole,
            scratch_shapes=[pltpu.VMEM((GROUP * 2 * LANES, rows), bf16)]
            + ([pltpu.VMEM((feats, rows), f32)] if final else []),
        ),
        compiler_params=params("arbitrary"),
        cost_estimate=cost(2 * 2 * half * 256 * feats * rows, half * 2 * feats * 512 * len(arrays) // 4),
        name="context_update" if pos else "update",
    )(base, meta, table_t, *arrays)


def absorb_kernel(width, ga0, ga1, gb0, gb1, ca0, ca1, cb0, cb1, in_ref, ctx_ref, c_out, x_out):
    @pl.when(pl.program_id(0) == 0)
    def _():
        c_out[...] = jnp.zeros_like(c_out)
        x_out[...] = jnp.zeros_like(x_out)

    group = ga0.shape[0]
    ga, gb = tokens_of(ga0, ga1), tokens_of(gb0, gb1)
    row = width - gb.shape[0]
    pos = gb[row:row + 1, :]
    grad = jnp.concatenate([ga, gb], axis=0)
    centre = jnp.concatenate([tokens_of(ca0, ca1), tokens_of(cb0, cb1)], axis=0) * pos
    feats = grad.shape[0]
    for value, ref, out in ((grad, in_ref, c_out), (centre, ctx_ref, x_out)):
        pairs = jnp.concatenate([ref[c, p] for p in range(group) for c in range(2)], axis=1)
        parts = jnp.concatenate(split3(value * learn_rate), axis=0)
        total = lax.dot_general(parts, pairs, NT, preferred_element_type=f32)
        out[...] += total[:feats] + total[feats:2 * feats] + total[2 * feats:]


def absorb(width, g, c, in_pairs, ctx_pairs):
    half, feats_half, n = g[0].shape
    piece = pl.BlockSpec((GROUP, feats_half, n), lambda p: (p, 0, 0))
    pair = pl.BlockSpec((2, GROUP, n, n), lambda p: (0, p, 0, 0))
    shape = jax.ShapeDtypeStruct((2 * feats_half, n), f32)
    spec = pl.BlockSpec((2 * feats_half, n), lambda p: (0, 0))
    return pl.pallas_call(
        functools.partial(absorb_kernel, width),
        out_shape=(shape, shape),
        grid=(half // GROUP,),
        in_specs=[piece] * 8 + [pair] * 2,
        out_specs=(spec, spec),
        compiler_params=params("arbitrary"),
        cost_estimate=cost(2 * 2 * 3 * half * 256 * feats_half * 2 * n, half * 256 * feats_half * 16),
        name="absorb",
    )(*g, *c, in_pairs, ctx_pairs)


def dot6(left, right, dims):
    m = left[0].shape[0]
    one = lax.dot_general(jnp.concatenate(left, axis=0), right[0], dims, preferred_element_type=f32)
    two = lax.dot_general(jnp.concatenate(left[:2], axis=0), right[1], dims, preferred_element_type=f32)
    three = lax.dot_general(left[0], right[2], dims, preferred_element_type=f32)
    return one[:m] + (one[m:2 * m] + two[:m]) + ((one[2 * m:] + two[m:]) + three)


def own_kernel(width, scale, slice_ref, c_ref, x_ref, denom_ref, meta_ref, a0, a1, b0, b1, out_ref, total):
    p = pl.program_id(0)

    @pl.when(p == 0)
    def _():
        total[...] = jnp.zeros_like(total)

    centre = c_ref[...]
    group, hot_slice = a0.shape[0], a0.shape[2]
    hot = jnp.concatenate([tokens_of(a0, a1), tokens_of(b0, b1)], axis=0)
    half = pl.num_programs(0) * group
    counts = [
        count_row(meta_ref.at[0], slice_ref[c * half + p * group + q], hot_slice)
        for q in range(group)
        for c in range(2)
    ]
    counts = jnp.concatenate(counts, axis=1)
    parts = split3(hot)
    scores = dot6(split3(centre.T), parts, NN)
    grad = (scale * counts) * jax.nn.sigmoid(scores)
    total[...] += dot6(parts, split3(grad), NT)

    @pl.when(p == pl.num_programs(0) - 1)
    def _():
        context = x_ref[...]
        positive = jnp.sum(centre * context, axis=0, keepdims=True)
        pos = jax.nn.sigmoid(positive) - 1.0
        grad = (pos * context + total[...]) / denom_ref[...]
        feature = lax.broadcasted_iota(i32, grad.shape, 0)
        out_ref[...] = jnp.where(feature == width, pos, grad)


def own_grads(width, scale, centre, context, denom, slice_of, meta, step, hot):
    feats, n = centre.shape
    half, feats_half, hot_slice = hot[0].shape
    group = max(1, 512 // hot_slice)
    whole = pl.BlockSpec((feats, n), lambda p, o: (0, 0))
    piece = pl.BlockSpec((group, feats_half, hot_slice), lambda p, o: (p, 0, 0))
    return pl.pallas_call(
        functools.partial(own_kernel, width, scale),
        out_shape=jax.ShapeDtypeStruct((feats, n), f32),
        grid_spec=pltpu.PrefetchScalarGridSpec(
            num_scalar_prefetch=1,
            grid=(half // group,),
            in_specs=[
                whole,
                whole,
                pl.BlockSpec((1, n), lambda p, o: (0, 0)),
                pl.BlockSpec((1, META, LANES), lambda p, o: (step, 0, 0)),
            ]
            + [piece] * 4,
            out_specs=whole,
            scratch_shapes=[pltpu.VMEM((feats, n), f32)],
        ),
        compiler_params=params("arbitrary"),
        cost_estimate=cost(2 * 2 * 6 * half * 2 * hot_slice * feats * n, half * 4 * feats_half * hot_slice * 4),
        name="own_grads",
    )(slice_of, centre, context, denom, meta, *hot)


def hot_kernel(scale, slice_ref, meta_ref, hot_a, hot_b, a, b, *refs):
    p = pl.program_id(0)
    total, parts = refs[-2:]
    first = len(refs) == 3

    @pl.when(p == 0)
    def _():
        total[...] = jnp.zeros_like(total) if first else refs[0][...]
        hot = jnp.concatenate([hot_a[0], hot_b[0]], axis=0)
        for k, part in enumerate(split3(hot)):
            parts[k] = part

    group, n = a.shape[0], a.shape[2]
    hot_slice = hot_a.shape[2]
    centre = jnp.concatenate(
        [jnp.concatenate([r[q] for q in range(group)], axis=1) for r in (a, b)], axis=0
    )
    scores = dot6(split3(centre.T), [parts[0], parts[1], parts[2]], NN)
    sums = []
    for q in range(0, group, 2):
        grads = []
        for r in (q, q + 1):
            counts = count_row(meta_ref.at[0, r, 0], slice_ref[0], hot_slice)
            grads.append((scale * counts) * jax.nn.sigmoid(scores[r * n:(r + 1) * n]))
        sums.append(dot6(split3(centre[:, q * n:(q + 2) * n]), split3(jnp.concatenate(grads, axis=0)), NN))
    while len(sums) > 1:
        sums = [x + y for x, y in zip(sums[::2], sums[1::2])]
    total[...] += sums[0]

    @pl.when(p == pl.num_programs(0) - 1)
    def _():
        if first:
            refs[0][...] = total[...]
        else:
            out_a, out_b = refs[1:3]
            h = out_a.shape[0]
            out_a[...] = hot_a[0] - learn_rate * total[:h, :]
            out_b[...] = hot_b[0] - learn_rate * total[h:, :]


def hot_update(scale, me_x, meta, step, hot, core, a, b, partial=None):
    half, feats_half, n = a.shape
    hot_slice = hot[0].shape[2]
    group = 2 * GROUP
    whole = pl.BlockSpec((2 * feats_half, hot_slice), lambda p, o: (0, 0))
    out = pl.BlockSpec((feats_half, hot_slice), lambda p, o: (0, 0))
    first = pl.BlockSpec((1, feats_half, hot_slice), lambda p, o: (0, 0, 0))
    piece = pl.BlockSpec((group, feats_half, n), lambda p, o: (p, 0, 0))
    sum_shape = jax.ShapeDtypeStruct((2 * feats_half, hot_slice), f32)
    half_shape = jax.ShapeDtypeStruct((feats_half, hot_slice), f32)
    return pl.pallas_call(
        functools.partial(hot_kernel, scale),
        out_shape=sum_shape if partial is None else (half_shape, half_shape),
        grid_spec=pltpu.PrefetchScalarGridSpec(
            num_scalar_prefetch=1,
            grid=(half // group,),
            in_specs=[
                pl.BlockSpec((1, group, 1, META, LANES), lambda p, o: (core, p, step, 0, 0)),
                first,
                first,
                piece,
                piece,
            ]
            + ([] if partial is None else [whole]),
            out_specs=whole if partial is None else (out, out),
            scratch_shapes=[
                pltpu.VMEM((2 * feats_half, hot_slice), f32),
                pltpu.VMEM((3, 2 * feats_half, hot_slice), bf16),
            ],
        ),
        compiler_params=params("arbitrary"),
        cost_estimate=cost(2 * 2 * 6 * half * 128 * hot_slice * feats_half * 2, half * 128 * feats_half * 8),
        name="hot_update",
    )(me_x, meta, hot[0], hot[2], a, b, *([] if partial is None else [partial]))


def spread_kernel(slice_ref, row0, row1, a0, a1, b0, b1):
    h = a0.shape[1]
    for row, a, b in ((row0, a0, b0), (row1, a1, b1)):
        turned = row[...].T
        a[0] = turned[:h]
        b[...] = jnp.zeros_like(b)
        b[0, :turned.shape[0] - h, :] = turned[h:]


def spread(hot_table, slice_of, feats):
    hot_rows, width = hot_table.shape
    count_of = slice_of.shape[0]
    half, hot_slice = count_of // 2, hot_rows // count_of
    shape = jax.ShapeDtypeStruct((half, feats // 2, hot_slice), f32)
    piece = pl.BlockSpec((1, feats // 2, hot_slice), lambda p, o: (p, 0, 0))
    return list(
        pl.pallas_call(
            spread_kernel,
            out_shape=(shape,) * 4,
            grid_spec=pltpu.PrefetchScalarGridSpec(
                num_scalar_prefetch=1,
                grid=(half,),
                in_specs=[
                    pl.BlockSpec((hot_slice, width), lambda p, o: (o[p], 0)),
                    pl.BlockSpec((hot_slice, width), lambda p, o: (o[half + p], 0)),
                ],
                out_specs=(piece,) * 4,
            ),
            compiler_params=params("arbitrary"),
            cost_estimate=cost(1e6, 2 * hot_rows * feats * 4),
            name="spread",
        )(slice_of, hot_table, hot_table)
    )


def collect_kernel(width, slice_ref, a0, a1, b0, b1, out):
    for c, (a, b) in enumerate(((a0, b0), (a1, b1))):

        @pl.when(pl.program_id(0) == c)
        def _():
            out[...] = jnp.concatenate([a[0], b[0]], axis=0).T[:, :width]


def collect(pieces, slice_of, width):
    half, feats_half, hot_slice = pieces[0].shape
    piece = pl.BlockSpec((1, feats_half, hot_slice), lambda c, p, o: (p, 0, 0))
    return pl.pallas_call(
        functools.partial(collect_kernel, width),
        out_shape=jax.ShapeDtypeStruct((2 * half * hot_slice, width), f32),
        grid_spec=pltpu.PrefetchScalarGridSpec(
            num_scalar_prefetch=1,
            grid=(2, half),
            in_specs=[piece] * 4,
            out_specs=pl.BlockSpec((hot_slice, width), lambda c, p, o: (o[c * half + p], 0)),
        ),
        compiler_params=pltpu.CompilerParams(
            dimension_semantics=("arbitrary", "arbitrary"), vmem_limit_bytes=62 * 2**20
        ),
        cost_estimate=cost(1e6, 4 * half * feats_half * hot_slice * 8),
        name="collect",
    )(slice_of, *pieces)


def rows_to_send(tree, me, out_table, ids, cap):
    rows = out_table.shape[0]
    devices, steps, n = ids.shape
    ids = ids - me * rows
    mine = (ids >= 0) & (ids < rows)
    before = jnp.triu(jnp.ones((n, n), bf16), 1)
    rank = jnp.dot(mine.astype(bf16), before, preferred_element_type=f32).astype(i32)
    slots = jnp.arange(cap, dtype=i32)
    hit = mine[:, :, None, :] & (rank[:, :, None, :] == slots[None, None, :, None])
    wanted = jnp.sum(jnp.where(hit, ids[:, :, None, :], 0), axis=3)
    order = tree.place_of(me ^ jnp.arange(devices, dtype=i32))
    return out_table[wanted[order].reshape(devices, steps * cap)]


def rows_that_came(got, owner, cap):
    steps, n = owner.shape
    same = (owner[:, :, None] == owner[:, None, :]) & (
        jnp.arange(n)[None, :, None] > jnp.arange(n)[None, None, :]
    )
    own_rank = jnp.sum(same.astype(i32), axis=2)
    at = (owner * steps + jnp.arange(steps, dtype=i32)[:, None]) * cap + own_rank
    return got.reshape(-1, got.shape[2])[at]


def body(
    in_table,
    out_table,
    hot_table,
    centre_owner,
    centre_row,
    bag_owner,
    bag_row,
    bag_len,
    context_owner,
    context_row,
    negative_ids,
):
    gx, gy = lax.axis_size("gx"), lax.axis_size("gy")
    tree = Tree(gx, gy)
    devices = tree.devices
    me_x = lax.axis_index("gx").astype(i32)
    me = me_x * gy + lax.axis_index("gy").astype(i32)
    steps, n, bag = bag_row.shape
    rows, width = in_table.shape
    out_rows = out_table.shape[0]
    hot_rows = hot_table.shape[0]
    neg = negative_ids.shape[1]
    cap = max(2, 2 * n // devices)
    hot_slice = hot_rows // gx
    feats = -(-(width + 1) // 16) * 16
    h = feats // 2
    scale = 16.0 / neg

    kept = jnp.arange(bag, dtype=i32)[None, None, :] < bag_len[:, :, None]
    centre_ids = centre_owner * rows + centre_row[:, :, None]
    bag_ids = bag_owner * rows + bag_row
    context_ids = context_owner * out_rows + context_row[:, :, None]
    own = jnp.concatenate([centre_ids, jnp.where(kept, bag_ids, -2), context_ids], axis=2)
    sent = jnp.concatenate([centre_ids, jnp.where(kept, bag_ids, -1), context_ids], axis=2)
    meta = jnp.concatenate([jnp.swapaxes(sent, 1, 2), count(negative_ids, hot_rows)], axis=1)
    span = len(tree.low) + len(tree.high) + 1
    short = len(tree.high) + 1
    lane = Lane(tree.gather_one(meta.reshape(steps * META, LANES)), span)
    while lane.left:
        stage([lane])
    meta_flat = lane.result.reshape(devices, steps, META, LANES)
    meta_all = meta_flat.reshape(2, devices // 2, steps, META, LANES)

    small = devices > 64
    in_base = (me * rows).reshape(1)
    out_base = (me * out_rows).reshape(1)
    spare = ((0, feats - width), (0, 0))
    in_t = jnp.pad(in_table.T, spare)
    source = in_t
    part = base_sums(source, meta_all, in_base, 0)
    hot_late, out_late = after((hot_table, out_table), part[0])
    out_t = jnp.pad(out_late.T, spare)
    slice_of = me_x ^ tree.slice_mask(jnp.arange(gx, dtype=i32))
    hot = spread(hot_late, slice_of, feats)
    denom = 1.0 + bag_len.astype(f32)

    def sums(s):
        return lambda gate: base_sums(gate(source), meta_all, in_base, s)

    def pair(later, e):
        return lambda gate: couple(gate(own), meta_all, later, e)

    def run(lanes, fills, kept, until):
        while until.left:
            name, fill = fills.pop(0) if fills else (None, None)
            beside = stage(lanes, fill)
            if name is not None:
                kept[name] = beside

    def requests(gate):
        return rows_to_send(tree, me, gate(out_table), meta_flat[:, :, SLOTS - 1, :], cap)

    kept = {}
    lane = Lane(tree.reduce(*part), span)
    fills = [(("rows",), requests)]
    if not small and steps > 1:
        fills.insert(0, (("sums", 1), sums(1)))
    run([lane], fills, kept, lane)
    base = [lane.result] + [None] * (steps - 1)
    send_rows = kept.pop(("rows",))
    owner = context_owner[:, :, 0]

    def exchange(rows, owner):
        got = lax.all_to_all(rows, axes, split_axis=0, concat_axis=0, tiled=True)
        got = rows_that_came(got, owner, cap)
        return [jnp.pad(got[k].T, spare) for k in range(owner.shape[0])]

    context = exchange(send_rows[:, :cap], owner[:1])
    real = jnp.arange(feats)[:, None] < width
    held = []
    added = [[] for _ in range(steps)]
    tables = [in_t, out_t]

    def grow(s, which):
        def fill(gate):
            g, c = held[s]
            final = s + 1 == steps
            if which == 0:
                return update(gate(tables[0]), meta_all, in_base, s, width, g, (), final)
            return update(gate(tables[1]), meta_all, out_base, s, width, c, g[2:], final)

        return fill

    def soak(later, e):
        def fill(gate):
            g, c = held[e]
            return absorb(width, [gate(g[0])] + g[1:], c, *kept[("pair", later, e)])

        return fill

    for s in range(steps):
        last = s + 1 == steps
        centre = jnp.where(real, base[s] / denom[s][None, :], 0.0)
        c_lane = Lane(tree.gather(centre), span)
        g = stage(
            [c_lane],
            lambda gate: own_grads(
                width, scale, gate(centre), context[s], denom[s][None, :], slice_of, meta, s, hot
            ),
        )
        g_lane = Lane(tree.gather(g), span)
        fills = []
        if not small:
            if s > 0:
                fills.append((("table", 1), grow(s - 1, 1)))
            if not last:
                fills.append((("pair", s + 1, s), pair(s + 1, s)))
            for later in range(s + 2, steps):
                fills.append((("pair", later, s), pair(later, s)))
            if s + 2 < steps:
                fills.append((("sums", s + 2), sums(s + 2)))
            if s > 0:
                fills.append((("table", 0), grow(s - 1, 0)))
        if len(fills) == 2:
            fills.insert(1, (None, None))
        r_lane = None
        while c_lane.left:
            if c_lane.left == 1:
                kept.update((name, fill(lambda x: x)) for name, fill in fills if name is not None)
                if not small and not last:
                    r_lane = Lane(tree.reduce(*kept.pop(("sums", s + 1))), span)
                half_sum = stage(
                    [c_lane, g_lane, r_lane],
                    lambda gate: hot_update(
                        scale, me_x.reshape(1), meta_all, s, hot, 0, gate(c_lane.sent[0]), c_lane.sent[1]
                    ),
                )
                continue
            if c_lane.left == 2 and s == 0 and not last:
                context += exchange(after(send_rows[:, cap:], c_lane.sent), owner[1:])
            name, fill = fills.pop(0) if fills else (None, None)
            beside = stage([c_lane, g_lane, r_lane], fill)
            if name is not None:
                kept[name] = beside
        for which in (0, 1):
            tables[which] = kept.pop(("table", which), tables[which])
        c = c_lane.result
        new_a, new_b = stage(
            [g_lane, r_lane],
            lambda gate: hot_update(scale, me_x.reshape(1), meta_all, s, hot, 1, gate(c[1]), c[3], half_sum),
        )
        while g_lane.left:
            stage([g_lane, r_lane])
        held.append((g_lane.result, c))
        h_lane = Lane(tree.gather_gx(new_a[None], new_b[None]), short)
        due = [(later, s) for later in range(s + 1, steps)]
        if small:
            for later, e in due:
                kept[("pair", later, e)] = couple(own, meta_all, later, e)
        fills = [(("soak", later, e), soak(later, e)) for later, e in due]
        if last or small:
            fills += [(("table", 1), grow(s, 1)), (("table", 0), grow(s, 0))]
        run([h_lane, r_lane], fills, kept, h_lane)
        for name, fill in fills:
            kept[name] = fill(lambda x: x)
        for which in (0, 1):
            tables[which] = kept.pop(("table", which), tables[which])
        for later, e in due:
            added[later].append(kept.pop(("soak", later, e)))
        hot = h_lane.result
        if not last:
            if small:
                source, tables, hot, context, added = lax.optimization_barrier(
                    (source, tables, hot, context, added)
                )
                r_lane = Lane(tree.reduce(*base_sums(source, meta_all, in_base, s + 1)), span)
            while r_lane.left:
                stage([r_lane])
            base[s + 1] = r_lane.result
            for centre_add, context_add in added[s + 1]:
                base[s + 1] = base[s + 1] - centre_add
                context[s + 1] = context[s + 1] - context_add
    return tables[0], tables[1], collect(hot, slice_of, width)


def solution(mesh):
    placed = (
        P(axes, None),
        P(axes, None),
        P(),
        P(None, axes, None),
        P(None, axes),
        P(None, axes, None),
        P(None, axes, None),
        P(None, axes),
        P(None, axes, None),
        P(None, axes),
        P(None, axes),
    )
    return jax.shard_map(
        body,
        mesh=mesh,
        in_specs=placed,
        out_specs=(P(axes, None), P(axes, None), P()),
        check_vma=False,
    )
```

```python
import functools
import jax
import jax.numpy as jnp
from jax import lax
from jax.experimental import pallas as pl
from jax.experimental.pallas import tpu as pltpu
from jax.sharding import PartitionSpec as P

learn_rate = 2.0
exact = lax.Precision.HIGHEST
axes = ("gx", "gy")
LANES = 128
SLOTS = 8
META = SLOTS + 16
GROUP = 4
f32, bf16, i32 = jnp.float32, jnp.bfloat16, jnp.int32
NN = (((1,), (0,)), ((), ()))
NT = (((1,), (1,)), ((), ()))
TN = (((0,), (0,)), ((), ()))


def swap(x, bit, devices):
    return lax.ppermute(x, axes, [(d, d ^ bit) for d in range(devices)])


def split3(x):
    hi = x.astype(bf16)
    rest = x - hi.astype(f32)
    mid = rest.astype(bf16)
    return hi, mid, (rest - mid.astype(f32)).astype(bf16)


def split2(x):
    hi = x.astype(bf16)
    return hi, (x - hi.astype(f32)).astype(bf16)


class Tree:
    def __init__(self, gx, gy):
        self.gx, self.gy = gx, gy
        self.devices = gx * gy
        self.low = [1 << b for b in range(gy.bit_length() - 1)]
        self.high = [gy << b for b in range(1, gx.bit_length() - 1)]
        self.core = gy

    def widen(self, parts, plans):
        m = len(plans[0])
        tails = [p.shape for p in parts]
        parts = [p.reshape((1,) * m + p.shape) for p in parts]
        for k in range(m):
            got = yield parts, [swap(p, plan[k][0], self.devices) for p, plan in zip(parts, plans)]
            parts = [jnp.concatenate([p, g], axis=plan[k][1]) for p, g, plan in zip(parts, got, plans)]
        return [p.reshape((-1,) + t) for p, t in zip(parts, tails)]

    def plans(self):
        mh, ml = len(self.high), len(self.low)
        low = [(self.low[b], ml - 1 - b) for b in reversed(range(ml))]
        high = [(self.high[b], mh - 1 - b) for b in range(mh)]
        return low, [high, high[::-1]]

    def gather(self, x):
        low, _ = self.plans()
        (x,) = yield from self.widen([x], [low])
        h = x.shape[1] // 2
        return (yield from self.gather_gx(x[:, :h], x[:, h:]))

    def gather_gx(self, a, b):
        _, high = self.plans()
        x, y = yield from self.widen([a, b], high)
        x, y = [v.reshape((-1,) + v.shape[2:]) for v in (x, y)]
        got = yield [x, y], [swap(x, self.core, self.devices), swap(y, self.core, self.devices)]
        return [x, got[0], y, got[1]]

    def gather_one(self, x):
        low, high = self.plans()
        (x,) = yield from self.widen([x], [low])
        (x,) = yield from self.widen([x], high[:1])
        x = x.reshape((-1,) + x.shape[2:])
        got = yield [x], [swap(x, self.core, self.devices)]
        return jnp.concatenate([x, got[0]], axis=0)

    def reduce(self, a0, a1, b0, b1):
        got = yield [a1, b1], [swap(a1, self.core, self.devices), swap(b1, self.core, self.devices)]
        low, high = self.plans()
        shape = (2,) * len(high[0]) + (self.gy,) + a0.shape[1:]
        parts = [(a0 + got[0]).reshape(shape), (b0 + got[1]).reshape(shape)]
        parts = yield from self.fold(parts, [plan[::-1] for plan in high])
        x = jnp.concatenate([p.reshape(p.shape[-3:]) for p in parts], axis=1)
        (x,) = yield from self.fold([x.reshape((2,) * len(low) + x.shape[1:])], [low[::-1]])
        return x.reshape(x.shape[-2:])

    def fold(self, parts, plans):
        for k in range(len(plans[0])):
            near = [lax.slice_in_dim(p, 0, 1, axis=plan[k][1]) for p, plan in zip(parts, plans)]
            far = [lax.slice_in_dim(p, 1, 2, axis=plan[k][1]) for p, plan in zip(parts, plans)]
            got = yield far, [swap(p, plan[k][0], self.devices) for p, plan in zip(far, plans)]
            parts = [p + g for p, g in zip(near, got)]
        return parts

    def place_of(self, mask):
        bits = self.devices.bit_length() - 1
        g, low = mask // self.gy, mask % self.gy
        return (g % 2) * (1 << (bits - 1)) + (g // 2) * self.gy + low

    def slice_mask(self, place):
        half = self.gx // 2
        return place // half + 2 * (place % half)


def params(*semantics):
    return pltpu.CompilerParams(dimension_semantics=semantics, vmem_limit_bytes=40 * 2**20)


def cost(flops, nbytes, trans=0):
    return pl.CostEstimate(flops=int(flops), bytes_accessed=int(nbytes), transcendentals=int(trans))


def after(x, *earlier):
    return lax.optimization_barrier((x, earlier))[0]


class Lane:
    def __init__(self, chain, stages):
        self.chain, self.left = chain, stages
        self.sent, self.got = next(chain)


def stage(lanes, fill=None):
    lanes = [lane for lane in lanes if lane is not None and lane.left > 0]
    sent = [lane.sent for lane in lanes]
    beside = fill(lambda x: after(x, sent)) if fill is not None else ()
    got, beside = lax.optimization_barrier(([lane.got for lane in lanes], beside))
    for lane, arrived in zip(lanes, got):
        lane.left -= 1
        try:
            lane.sent, lane.got = lane.chain.send(arrived)
        except StopIteration as end:
            lane.result = end.value
    return beside


def count_kernel(ids_ref, out_ref):
    groups = out_ref.shape[1]
    for s in range(out_ref.shape[0]):
        ids = ids_ref[s:s + 1, :]
        n = ids.shape[1]
        high = jnp.where(lax.broadcasted_iota(i32, (groups, n), 0) == ids // LANES, 1.0, 0.0)
        low = jnp.where(lax.broadcasted_iota(i32, (LANES, n), 0) == ids % LANES, 1.0, 0.0)
        total = lax.dot_general(high.astype(bf16), low.astype(bf16), NT, preferred_element_type=f32)
        out_ref[s] = total.astype(i32)


def count(ids, hot_rows):
    return pl.pallas_call(
        count_kernel,
        out_shape=jax.ShapeDtypeStruct((ids.shape[0], hot_rows // LANES, LANES), i32),
        compiler_params=pltpu.CompilerParams(vmem_limit_bytes=40 * 2**20),
        cost_estimate=cost(1e6, 1e5),
        name="count",
    )(ids)


def count_row(rows_ref, slice_at, width):
    at = SLOTS + slice_at * (width // LANES)
    rows = [rows_ref[pl.ds(at + q, 1), :] for q in range(width // LANES)]
    return jnp.concatenate(rows, axis=1).astype(f32)


def couple_kernel(own_ref, other_ref, in_ref, out_ref, wide):
    @pl.when(pl.program_id(0) == 0)
    def _():
        for k in range(SLOTS):
            wide[k] = jnp.broadcast_to(own_ref[0, :, k:k + 1], wide.shape[1:])

    for c in range(2):
        total = jnp.zeros(wide.shape[1:], f32)
        for k in range(SLOTS - 1):
            row = other_ref[c, 0, 0, k:k + 1, :]
            in_bag = wide[1] == row
            for j in range(2, SLOTS - 1):
                in_bag = in_bag | (wide[j] == row)
            total = total + jnp.where(in_bag, 1.0, 0.0) + jnp.where(wide[0] == row, 1.0, 0.0)
        in_ref[c, 0] = total.astype(bf16)
        same = wide[SLOTS - 1] == other_ref[c, 0, 0, SLOTS - 1:SLOTS, :]
        out_ref[c, 0] = jnp.where(same, 1.0, 0.0).astype(bf16)


def couple(own, meta, later, earlier):
    half, n = meta.shape[1], own.shape[1]
    shape = jax.ShapeDtypeStruct((2, half, n, n), bf16)
    spec = pl.BlockSpec((2, 1, n, n), lambda p: (0, p, 0, 0))
    return pl.pallas_call(
        couple_kernel,
        out_shape=(shape, shape),
        grid=(half,),
        in_specs=[
            pl.BlockSpec((1, n, SLOTS), lambda p: (later, 0, 0)),
            pl.BlockSpec((2, 1, 1, META, LANES), lambda p: (0, p, earlier, 0, 0)),
        ],
        out_specs=(spec, spec),
        scratch_shapes=[pltpu.VMEM((SLOTS, n, n), i32)],
        compiler_params=params("arbitrary"),
        cost_estimate=cost(half * 2 * n * n * 150, half * n * n * 8),
        name="couple",
    )(own, meta)


def local_rows(ids, rows, context):
    if context:
        return [ids[SLOTS - 1:SLOTS, :]]
    ids = jnp.where((ids >= 0) & (ids < rows), ids, -1)
    return [ids[0:1, :], jnp.max(ids[1:SLOTS - 1, :], axis=0, keepdims=True)]


def base_kernel(rows, base_ref, meta_ref, table_ref, a0, a1, b0, b1, parts):
    feats = table_ref.shape[0]

    @pl.when(pl.program_id(0) == 0)
    def _():
        for k, part in enumerate(split3(table_ref[...])):
            parts[k * feats:(k + 1) * feats, :] = part

    h = a0.shape[1]
    iota = lax.broadcasted_iota(i32, (rows, LANES), 0)
    for p in range(a0.shape[0]):
        picks = []
        for c in range(2):
            one, two = local_rows(meta_ref[c, p, 0, :SLOTS, :] - base_ref[0], rows, False)
            picks.append(jnp.where(iota == one, 1.0, 0.0) + jnp.where(iota == two, 1.0, 0.0))
        pick = jnp.concatenate(picks, axis=1).astype(bf16)
        total = jnp.dot(parts[...], pick, preferred_element_type=f32)
        total = total[:feats] + total[feats:2 * feats] + total[2 * feats:]
        a0[p] = total[:h, :LANES]
        a1[p] = total[:h, LANES:]
        b0[p] = total[h:, :LANES]
        b1[p] = total[h:, LANES:]


def base_sums(table_t, meta, base, step):
    half = meta.shape[1]
    feats, rows = table_t.shape
    shape = jax.ShapeDtypeStruct((half, feats // 2, LANES), f32)
    spec = pl.BlockSpec((GROUP, feats // 2, LANES), lambda p, b: (p, 0, 0))
    return pl.pallas_call(
        functools.partial(base_kernel, rows),
        out_shape=(shape,) * 4,
        grid_spec=pltpu.PrefetchScalarGridSpec(
            num_scalar_prefetch=1,
            grid=(half // GROUP,),
            in_specs=[
                pl.BlockSpec((2, GROUP, 1, META, LANES), lambda p, b: (0, p, step, 0, 0)),
                pl.BlockSpec((feats, rows), lambda p, b: (0, 0)),
            ],
            out_specs=(spec,) * 4,
            scratch_shapes=[pltpu.VMEM((3 * feats, rows), bf16)],
        ),
        compiler_params=params("arbitrary"),
        cost_estimate=cost(2 * 3 * half * 256 * feats * rows, half * 2 * feats * 512 + feats * rows * 4),
        name="base_sums",
    )(base, meta, table_t)


def tokens_of(r0, r1):
    return jnp.concatenate([r[p] for p in range(r0.shape[0]) for r in (r0, r1)], axis=1)


def update_kernel(rows, width, context, final, base_ref, meta_ref, table_ref, *refs):
    if final:
        result, pick, out_ref = refs[-3:]
    else:
        out_ref, pick = refs[-2:]
    ga0, ga1, gb0, gb1 = refs[:4]

    @pl.when(pl.program_id(0) == 0)
    def _():
        out_ref[...] = table_ref[...]

    iota = lax.broadcasted_iota(i32, (LANES, rows), 1)
    for p in range(ga0.shape[0]):
        for c in range(2):
            ids = meta_ref[c, p, 0, :SLOTS, :] - base_ref[0]
            found = local_rows(ids, rows, context)
            found = jnp.concatenate(found + [found[0]] * (SLOTS - len(found)), axis=0).T
            hits = jnp.where(iota == found[:, 0:1], 1.0, 0.0)
            if not context:
                hits = hits + jnp.where(iota == found[:, 1:2], 1.0, 0.0)
            at = (2 * p + c) * LANES
            pick[at:at + LANES, :] = hits.astype(bf16)
    ga, gb = tokens_of(ga0, ga1), tokens_of(gb0, gb1)
    if context:
        pos0, pos1 = refs[4], refs[5]
        row = width - gb.shape[0]
        pos = jnp.concatenate(
            [r[p, row:row + 1, :] for p in range(pos0.shape[0]) for r in (pos0, pos1)], axis=1
        )
        ga, gb = ga * pos, gb * pos
    grad = jnp.concatenate([ga, gb], axis=0) * learn_rate
    feats = grad.shape[0]
    both = jnp.concatenate(split2(grad), axis=0)
    total = jnp.dot(both, pick[...], preferred_element_type=f32)
    out_ref[...] = out_ref[...] - (total[:feats] + total[feats:])
    if final:

        @pl.when(pl.program_id(0) == pl.num_programs(0) - 1)
        def _():
            result[...] = out_ref[...].T[:, :width]


def update(table_t, meta, base, step, width, g, pos=(), final=False):
    half = meta.shape[1]
    feats, rows = table_t.shape
    piece = pl.BlockSpec((GROUP, feats // 2, LANES), lambda p, b: (p, 0, 0))
    whole = pl.BlockSpec((feats, rows), lambda p, b: (0, 0))
    arrays = list(g) + list(pos)
    return pl.pallas_call(
        functools.partial(update_kernel, rows, width, bool(pos), final),
        out_shape=jax.ShapeDtypeStruct((rows, width) if final else (feats, rows), f32),
        grid_spec=pltpu.PrefetchScalarGridSpec(
            num_scalar_prefetch=1,
            grid=(half // GROUP,),
            in_specs=[pl.BlockSpec((2, GROUP, 1, META, LANES), lambda p, b: (0, p, step, 0, 0)), whole]
            + [piece] * len(arrays),
            out_specs=pl.BlockSpec((rows, width), lambda p, b: (0, 0)) if final else whole,
            scratch_shapes=[pltpu.VMEM((GROUP * 2 * LANES, rows), bf16)]
            + ([pltpu.VMEM((feats, rows), f32)] if final else []),
        ),
        compiler_params=params("arbitrary"),
        cost_estimate=cost(2 * 2 * half * 256 * feats * rows, half * 2 * feats * 512 * len(arrays) // 4),
        name="context_update" if pos else "update",
    )(base, meta, table_t, *arrays)


def absorb_kernel(width, ga0, ga1, gb0, gb1, ca0, ca1, cb0, cb1, *refs):
    pairs, outs = refs[:len(refs) // 2], refs[len(refs) // 2:]

    @pl.when(pl.program_id(0) == 0)
    def _():
        for out in outs:
            out[...] = jnp.zeros_like(out)

    group = ga0.shape[0]
    ga, gb = tokens_of(ga0, ga1), tokens_of(gb0, gb1)
    row = width - gb.shape[0]
    pos = gb[row:row + 1, :]
    grad = jnp.concatenate([ga, gb], axis=0)
    centre = jnp.concatenate([tokens_of(ca0, ca1), tokens_of(cb0, cb1)], axis=0) * pos
    feats = grad.shape[0]
    for k, value in enumerate((grad, centre)):
        parts = jnp.concatenate(split3(value * learn_rate), axis=0)
        for ref, out in zip(pairs[k::2], outs[k::2]):
            both = jnp.concatenate([ref[c, p] for p in range(group) for c in range(2)], axis=1)
            total = lax.dot_general(parts, both, NT, preferred_element_type=f32)
            out[...] += total[:feats] + total[feats:2 * feats] + total[2 * feats:]


def absorb(width, g, c, pairs):
    half, feats_half, n = g[0].shape
    piece = pl.BlockSpec((GROUP, feats_half, n), lambda p: (p, 0, 0))
    pair = pl.BlockSpec((2, GROUP, n, n), lambda p: (0, p, 0, 0))
    shape = jax.ShapeDtypeStruct((2 * feats_half, n), f32)
    spec = pl.BlockSpec((2 * feats_half, n), lambda p: (0, 0))
    number = 2 * len(pairs)
    outs = pl.pallas_call(
        functools.partial(absorb_kernel, width),
        out_shape=(shape,) * number,
        grid=(half // GROUP,),
        in_specs=[piece] * 8 + [pair] * number,
        out_specs=(spec,) * number,
        compiler_params=params("arbitrary"),
        cost_estimate=cost(2 * 3 * number * half * 256 * feats_half * 2 * n, half * 256 * feats_half * 16),
        name="absorb",
    )(*g, *c, *[array for both in pairs for array in both])
    return [(outs[k], outs[k + 1]) for k in range(0, number, 2)]


def dot6(left, right, dims):
    m = left[0].shape[0]
    one = lax.dot_general(jnp.concatenate(left, axis=0), right[0], dims, preferred_element_type=f32)
    two = lax.dot_general(jnp.concatenate(left[:2], axis=0), right[1], dims, preferred_element_type=f32)
    three = lax.dot_general(left[0], right[2], dims, preferred_element_type=f32)
    return one[:m] + (one[m:2 * m] + two[:m]) + ((one[2 * m:] + two[m:]) + three)


def own_kernel(width, scale, slice_ref, c_ref, x_ref, denom_ref, meta_ref, a0, a1, b0, b1, out_ref, total):
    p = pl.program_id(0)

    @pl.when(p == 0)
    def _():
        total[...] = jnp.zeros_like(total)

    centre = c_ref[...]
    group, hot_slice = a0.shape[0], a0.shape[2]
    hot = jnp.concatenate([tokens_of(a0, a1), tokens_of(b0, b1)], axis=0)
    half = pl.num_programs(0) * group
    counts = [
        count_row(meta_ref.at[0], slice_ref[c * half + p * group + q], hot_slice)
        for q in range(group)
        for c in range(2)
    ]
    counts = jnp.concatenate(counts, axis=1)
    parts = split3(hot)
    scores = dot6(split3(centre.T), parts, NN)
    grad = (scale * counts) * jax.nn.sigmoid(scores)
    total[...] += dot6(parts, split3(grad), NT)

    @pl.when(p == pl.num_programs(0) - 1)
    def _():
        context = x_ref[...]
        positive = jnp.sum(centre * context, axis=0, keepdims=True)
        pos = jax.nn.sigmoid(positive) - 1.0
        grad = (pos * context + total[...]) / denom_ref[...]
        feature = lax.broadcasted_iota(i32, grad.shape, 0)
        out_ref[...] = jnp.where(feature == width, pos, grad)


def own_grads(width, scale, centre, context, denom, slice_of, meta, step, hot):
    feats, n = centre.shape
    half, feats_half, hot_slice = hot[0].shape
    group = max(1, 512 // hot_slice)
    whole = pl.BlockSpec((feats, n), lambda p, o: (0, 0))
    piece = pl.BlockSpec((group, feats_half, hot_slice), lambda p, o: (p, 0, 0))
    return pl.pallas_call(
        functools.partial(own_kernel, width, scale),
        out_shape=jax.ShapeDtypeStruct((feats, n), f32),
        grid_spec=pltpu.PrefetchScalarGridSpec(
            num_scalar_prefetch=1,
            grid=(half // group,),
            in_specs=[
                whole,
                whole,
                pl.BlockSpec((1, n), lambda p, o: (0, 0)),
                pl.BlockSpec((1, META, LANES), lambda p, o: (step, 0, 0)),
            ]
            + [piece] * 4,
            out_specs=whole,
            scratch_shapes=[pltpu.VMEM((feats, n), f32)],
        ),
        compiler_params=params("arbitrary"),
        cost_estimate=cost(2 * 2 * 6 * half * 2 * hot_slice * feats * n, half * 4 * feats_half * hot_slice * 4),
        name="own_grads",
    )(slice_of, centre, context, denom, meta, *hot)


def hot_kernel(scale, slice_ref, meta_ref, hot_a, hot_b, a, b, *refs):
    p = pl.program_id(0)
    total, parts = refs[-2:]
    first = len(refs) == 3

    @pl.when(p == 0)
    def _():
        total[...] = jnp.zeros_like(total) if first else refs[0][...]
        hot = jnp.concatenate([hot_a[0], hot_b[0]], axis=0)
        for k, part in enumerate(split3(hot)):
            parts[k] = part

    group, n = a.shape[0], a.shape[2]
    hot_slice = hot_a.shape[2]
    centre = jnp.concatenate(
        [jnp.concatenate([r[q] for q in range(group)], axis=1) for r in (a, b)], axis=0
    )
    scores = dot6(split3(centre.T), [parts[0], parts[1], parts[2]], NN)
    sums = []
    for q in range(0, group, 2):
        grads = []
        for r in (q, q + 1):
            counts = count_row(meta_ref.at[0, r, 0], slice_ref[0], hot_slice)
            grads.append((scale * counts) * jax.nn.sigmoid(scores[r * n:(r + 1) * n]))
        sums.append(dot6(split3(centre[:, q * n:(q + 2) * n]), split3(jnp.concatenate(grads, axis=0)), NN))
    while len(sums) > 1:
        sums = [x + y for x, y in zip(sums[::2], sums[1::2])]
    total[...] += sums[0]

    @pl.when(p == pl.num_programs(0) - 1)
    def _():
        if first:
            refs[0][...] = total[...]
        else:
            out_a, out_b = refs[1:3]
            h = out_a.shape[0]
            out_a[...] = hot_a[0] - learn_rate * total[:h, :]
            out_b[...] = hot_b[0] - learn_rate * total[h:, :]


def hot_update(scale, me_x, meta, step, hot, core, a, b, partial=None):
    half, feats_half, n = a.shape
    hot_slice = hot[0].shape[2]
    group = 2 * GROUP
    whole = pl.BlockSpec((2 * feats_half, hot_slice), lambda p, o: (0, 0))
    out = pl.BlockSpec((feats_half, hot_slice), lambda p, o: (0, 0))
    first = pl.BlockSpec((1, feats_half, hot_slice), lambda p, o: (0, 0, 0))
    piece = pl.BlockSpec((group, feats_half, n), lambda p, o: (p, 0, 0))
    sum_shape = jax.ShapeDtypeStruct((2 * feats_half, hot_slice), f32)
    half_shape = jax.ShapeDtypeStruct((feats_half, hot_slice), f32)
    return pl.pallas_call(
        functools.partial(hot_kernel, scale),
        out_shape=sum_shape if partial is None else (half_shape, half_shape),
        grid_spec=pltpu.PrefetchScalarGridSpec(
            num_scalar_prefetch=1,
            grid=(half // group,),
            in_specs=[
                pl.BlockSpec((1, group, 1, META, LANES), lambda p, o: (core, p, step, 0, 0)),
                first,
                first,
                piece,
                piece,
            ]
            + ([] if partial is None else [whole]),
            out_specs=whole if partial is None else (out, out),
            scratch_shapes=[
                pltpu.VMEM((2 * feats_half, hot_slice), f32),
                pltpu.VMEM((3, 2 * feats_half, hot_slice), bf16),
            ],
        ),
        compiler_params=params("arbitrary"),
        cost_estimate=cost(2 * 2 * 6 * half * 128 * hot_slice * feats_half * 2, half * 128 * feats_half * 8),
        name="hot_update",
    )(me_x, meta, hot[0], hot[2], a, b, *([] if partial is None else [partial]))


def spread_kernel(slice_ref, row0, row1, a0, a1, b0, b1):
    h = a0.shape[1]
    for row, a, b in ((row0, a0, b0), (row1, a1, b1)):
        turned = row[...].T
        a[0] = turned[:h]
        b[...] = jnp.zeros_like(b)
        b[0, :turned.shape[0] - h, :] = turned[h:]


def spread(hot_table, slice_of, feats):
    hot_rows, width = hot_table.shape
    count_of = slice_of.shape[0]
    half, hot_slice = count_of // 2, hot_rows // count_of
    shape = jax.ShapeDtypeStruct((half, feats // 2, hot_slice), f32)
    piece = pl.BlockSpec((1, feats // 2, hot_slice), lambda p, o: (p, 0, 0))
    return list(
        pl.pallas_call(
            spread_kernel,
            out_shape=(shape,) * 4,
            grid_spec=pltpu.PrefetchScalarGridSpec(
                num_scalar_prefetch=1,
                grid=(half,),
                in_specs=[
                    pl.BlockSpec((hot_slice, width), lambda p, o: (o[p], 0)),
                    pl.BlockSpec((hot_slice, width), lambda p, o: (o[half + p], 0)),
                ],
                out_specs=(piece,) * 4,
            ),
            compiler_params=params("arbitrary"),
            cost_estimate=cost(1e6, 2 * hot_rows * feats * 4),
            name="spread",
        )(slice_of, hot_table, hot_table)
    )


def collect_kernel(width, slice_ref, a0, a1, b0, b1, out):
    for c, (a, b) in enumerate(((a0, b0), (a1, b1))):

        @pl.when(pl.program_id(0) == c)
        def _():
            out[...] = jnp.concatenate([a[0], b[0]], axis=0).T[:, :width]


def collect(pieces, slice_of, width):
    half, feats_half, hot_slice = pieces[0].shape
    piece = pl.BlockSpec((1, feats_half, hot_slice), lambda c, p, o: (p, 0, 0))
    return pl.pallas_call(
        functools.partial(collect_kernel, width),
        out_shape=jax.ShapeDtypeStruct((2 * half * hot_slice, width), f32),
        grid_spec=pltpu.PrefetchScalarGridSpec(
            num_scalar_prefetch=1,
            grid=(2, half),
            in_specs=[piece] * 4,
            out_specs=pl.BlockSpec((hot_slice, width), lambda c, p, o: (o[c * half + p], 0)),
        ),
        compiler_params=params("arbitrary", "arbitrary"),
        cost_estimate=cost(1e6, 4 * half * feats_half * hot_slice * 8),
        name="collect",
    )(slice_of, *pieces)


def rows_to_send(tree, me, out_table, ids, cap):
    rows = out_table.shape[0]
    devices, steps, n = ids.shape
    ids = ids - me * rows
    mine = (ids >= 0) & (ids < rows)
    before = jnp.triu(jnp.ones((n, n), bf16), 1)
    rank = jnp.dot(mine.astype(bf16), before, preferred_element_type=f32).astype(i32)
    slots = jnp.arange(cap, dtype=i32)
    hit = mine[:, :, None, :] & (rank[:, :, None, :] == slots[None, None, :, None])
    wanted = jnp.sum(jnp.where(hit, ids[:, :, None, :], 0), axis=3)
    order = tree.place_of(me ^ jnp.arange(devices, dtype=i32))
    return out_table[wanted[order].reshape(devices, steps * cap)]


def rows_that_came(got, owner, cap):
    steps, n = owner.shape
    same = (owner[:, :, None] == owner[:, None, :]) & (
        jnp.arange(n)[None, :, None] > jnp.arange(n)[None, None, :]
    )
    own_rank = jnp.sum(same.astype(i32), axis=2)
    at = (owner * steps + jnp.arange(steps, dtype=i32)[:, None]) * cap + own_rank
    return got.reshape(-1, got.shape[2])[at]


def body(
    in_table,
    out_table,
    hot_table,
    centre_owner,
    centre_row,
    bag_owner,
    bag_row,
    bag_len,
    context_owner,
    context_row,
    negative_ids,
):
    gx, gy = lax.axis_size("gx"), lax.axis_size("gy")
    tree = Tree(gx, gy)
    devices = tree.devices
    me_x = lax.axis_index("gx").astype(i32)
    me = me_x * gy + lax.axis_index("gy").astype(i32)
    steps, n, bag = bag_row.shape
    rows, width = in_table.shape
    out_rows = out_table.shape[0]
    hot_rows = hot_table.shape[0]
    neg = negative_ids.shape[1]
    cap = max(2, 2 * n // devices)
    hot_slice = hot_rows // gx
    feats = -(-(width + 1) // 16) * 16
    h = feats // 2
    scale = 16.0 / neg

    kept = jnp.arange(bag, dtype=i32)[None, None, :] < bag_len[:, :, None]
    centre_ids = centre_owner * rows + centre_row[:, :, None]
    bag_ids = bag_owner * rows + bag_row
    context_ids = context_owner * out_rows + context_row[:, :, None]
    own = jnp.concatenate([centre_ids, jnp.where(kept, bag_ids, -2), context_ids], axis=2)
    sent = jnp.concatenate([centre_ids, jnp.where(kept, bag_ids, -1), context_ids], axis=2)
    meta = jnp.concatenate([jnp.swapaxes(sent, 1, 2), count(negative_ids, hot_rows)], axis=1)
    span = len(tree.low) + len(tree.high) + 1
    short = len(tree.high) + 1
    lane = Lane(tree.gather_one(meta.reshape(steps * META, LANES)), span)
    while lane.left:
        stage([lane])
    meta_flat = lane.result.reshape(devices, steps, META, LANES)
    meta_all = meta_flat.reshape(2, devices // 2, steps, META, LANES)

    small = devices > 64
    in_base = (me * rows).reshape(1)
    out_base = (me * out_rows).reshape(1)
    spare = ((0, feats - width), (0, 0))
    in_t = jnp.pad(in_table.T, spare)
    source = in_t
    part = base_sums(source, meta_all, in_base, 0)
    hot_late, out_late = after((hot_table, out_table), part[0])
    out_t = jnp.pad(out_late.T, spare)
    slice_of = me_x ^ tree.slice_mask(jnp.arange(gx, dtype=i32))
    hot = spread(hot_late, slice_of, feats)
    denom = 1.0 + bag_len.astype(f32)

    def sums(s):
        return lambda gate: base_sums(gate(source), meta_all, in_base, s)

    def pair(later, e):
        return lambda gate: couple(gate(own), meta_all, later, e)

    def run(lanes, fills, kept, until):
        while until.left:
            name, fill = fills.pop(0) if fills else (None, None)
            beside = stage(lanes, fill)
            if name is not None:
                kept[name] = beside

    def requests(gate):
        return rows_to_send(tree, me, gate(out_table), meta_flat[:, :, SLOTS - 1, :], cap)

    kept = {}
    lane = Lane(tree.reduce(*part), span)
    fills = [(("rows",), requests)]
    if not small and steps > 1:
        fills.insert(0, (("sums", 1), sums(1)))
    run([lane], fills, kept, lane)
    base = [lane.result] + [None] * (steps - 1)
    got = lax.all_to_all(kept.pop(("rows",)), axes, split_axis=0, concat_axis=0, tiled=True)
    got = rows_that_came(got, context_owner[:, :, 0], cap)
    context = [jnp.pad(got[k].T, spare) for k in range(steps)]
    real = jnp.arange(feats)[:, None] < width
    held = []
    added = [[] for _ in range(steps)]
    tables = [in_t, out_t]

    def grow(s, which):
        def fill(gate):
            g, c = held[s]
            final = s + 1 == steps
            if which == 0:
                return update(gate(tables[0]), meta_all, in_base, s, width, g, (), final)
            return update(gate(tables[1]), meta_all, out_base, s, width, c, g[2:], final)

        return fill

    def soak(e):
        def fill(gate):
            g, c = held[e]
            pairs = [kept[("pair", later, e)] for later in range(e + 1, steps)]
            return absorb(width, [gate(g[0])] + g[1:], c, pairs)

        return fill

    for s in range(steps):
        last = s + 1 == steps
        centre = jnp.where(real, base[s] / denom[s][None, :], 0.0)
        c_lane = Lane(tree.gather(centre), span)
        g = stage(
            [c_lane],
            lambda gate: own_grads(
                width, scale, gate(centre), context[s], denom[s][None, :], slice_of, meta, s, hot
            ),
        )
        g_lane = Lane(tree.gather(g), span)
        fills = []
        if not small:
            if s > 0:
                fills.append((("table", 1), grow(s - 1, 1)))
            if not last:
                fills.append((("pair", s + 1, s), pair(s + 1, s)))
            for later in range(s + 2, steps):
                fills.append((("pair", later, s), pair(later, s)))
            if s + 2 < steps:
                fills.append((("sums", s + 2), sums(s + 2)))
            if s > 0:
                fills.append((("table", 0), grow(s - 1, 0)))
        if len(fills) == 2:
            fills.insert(1, (None, None))
        r_lane = None
        while c_lane.left:
            if c_lane.left == 1:
                kept.update((name, fill(lambda x: x)) for name, fill in fills if name is not None)
                if not small and not last:
                    r_lane = Lane(tree.reduce(*kept.pop(("sums", s + 1))), span)
                half_sum = stage(
                    [c_lane, g_lane, r_lane],
                    lambda gate: hot_update(
                        scale, me_x.reshape(1), meta_all, s, hot, 0, gate(c_lane.sent[0]), c_lane.sent[1]
                    ),
                )
                continue
            name, fill = fills.pop(0) if fills else (None, None)
            beside = stage([c_lane, g_lane, r_lane], fill)
            if name is not None:
                kept[name] = beside
        for which in (0, 1):
            tables[which] = kept.pop(("table", which), tables[which])
        c = c_lane.result
        new_a, new_b = stage(
            [g_lane, r_lane],
            lambda gate: hot_update(scale, me_x.reshape(1), meta_all, s, hot, 1, gate(c[1]), c[3], half_sum),
        )
        while g_lane.left:
            stage([g_lane, r_lane])
        held.append((g_lane.result, c))
        h_lane = Lane(tree.gather_gx(new_a[None], new_b[None]), short)
        due = [(later, s) for later in range(s + 1, steps)]
        if small:
            for later, e in due:
                kept[("pair", later, e)] = couple(own, meta_all, later, e)
        fills = [(("soak", s), soak(s))] if due else []
        if last or small:
            fills += [(("table", 1), grow(s, 1)), (("table", 0), grow(s, 0))]
        run([h_lane, r_lane], fills, kept, h_lane)
        for name, fill in fills:
            kept[name] = fill(lambda x: x)
        for which in (0, 1):
            tables[which] = kept.pop(("table", which), tables[which])
        for (later, _), both in zip(due, kept.pop(("soak", s), [])):
            added[later].append(both)
        hot = h_lane.result
        if not last:
            if small:
                source, tables, hot, context, added = lax.optimization_barrier(
                    (source, tables, hot, context, added)
                )
                r_lane = Lane(tree.reduce(*base_sums(source, meta_all, in_base, s + 1)), span)
            while r_lane.left:
                stage([r_lane])
            base[s + 1] = r_lane.result
            for centre_add, context_add in added[s + 1]:
                base[s + 1] = base[s + 1] - centre_add
                context[s + 1] = context[s + 1] - context_add
    return tables[0], tables[1], collect(hot, slice_of, width)


def solution(mesh):
    placed = (
        P(axes, None),
        P(axes, None),
        P(),
        P(None, axes, None),
        P(None, axes),
        P(None, axes, None),
        P(None, axes, None),
        P(None, axes),
        P(None, axes, None),
        P(None, axes),
        P(None, axes),
    )
    return jax.shard_map(
        body,
        mesh=mesh,
        in_specs=placed,
        out_specs=(P(axes, None), P(axes, None), P()),
        check_vma=False,
    )
```
